32 devices in a mesh: runs: 2 (over y), tm: 2 (over x), cells: 4 (over z), feat: 2 (over core).
Axes of the slice: x: 2, y: 2, z: 4, core: 2. Of those that a mesh axis runs over, the one named last changes fastest.
Arguments:
- principal_coordinates: bfloat16 [4, 64, 8192], P(('runs', 'tm'), None, ('cells', 'feat')), parts along dimension 0, may hold values from -6 to 6
- present_potentials: float32 [4, 8192], P(('runs', 'tm'), ('cells', 'feat')), parts along dimension 0, may hold values from 0.25 to 4
- destination_tiles: int32 [4, 32, 8], P(('runs', 'tm'), ('cells', 'feat')), parts along dimension 0, may hold values from 0 to 31, as said below
- living_totals: int32 [4], P('runs'), parts along dimension 0, may hold values from 4096 to 8192, as said below
Outputs:
- renewed_potentials: float32 [4, 8192], P(('runs', 'tm'), ('cells', 'feat')), parts along dimension 0
- prior_projections: float32 [4, 8192], P(('runs', 'tm'), ('cells', 'feat')), parts along dimension 0
The draws below stay inside these ranges and needn't reach their ends.
There are 2 independent parts, one for each index of `runs`. The reference program is written for one: setup_inputs(seed, part) draws one part's arguments, and reference() takes and returns one part's arrays. A program takes and returns all parts, laid end to end along the dimension named above; each array names one. Nothing has to cross between parts.
Inputs may be any that keep to these rules, and one draw needn't show every extreme that they name: `destination_tiles`: row b of time t lists 8 distinct blocks: 4 distinct values c below 16, b modulo 32/2 among them, each together with c + 16. The lists of the last time point are not used. The live cells of time t are its first living_totals[t] cells; in every draw one time point is full.
All inputs are finite; a program needn't handle non-finite values.
Results may differ from the reference program's by a relative error of at most 0.0003.
Values may be sent and summed in bfloat16 or wider, within the bound.
No kernel may reach another device: no remote copies, remote signals or barrier semaphores. Data moves between devices by JAX's collectives and lax.ppermute only.
A program may use at most 64 MiB of HBM per device.

```python
import math
import jax
import jax.numpy as jnp
from jax import lax

D = 64
BLK = 256
NB = 8
SNAPSHOT_COUNT = 2
SAMPLES_EACH_DAY = 8192
NBLK = 32


def draw_destination_tiles(key, part):
    key = jax.random.fold_in(key, 7)
    half_blocks = NBLK // 2
    pair_count = NB // 2
    shape_here = (SNAPSHOT_COUNT, NBLK, half_blocks - 1)
    rank_scores = jax.random.randint(key, shape_here, 0, 2 ** 16) * half_blocks + lax.broadcasted_iota(jnp.int32, shape_here, 2)
    ranking = jnp.argsort(rank_scores, axis=-1, stable=True).astype(jnp.int32)
    offsets = ranking[..., :pair_count - 1] + 1
    home_block = lax.broadcasted_iota(jnp.int32, (SNAPSHOT_COUNT, NBLK, 1), 1) % half_blocks
    base_blocks = jnp.concatenate([home_block, (home_block + offsets) % half_blocks], axis=-1)
    return jnp.concatenate([base_blocks, base_blocks + half_blocks], axis=-1).astype(jnp.int32)


def draw_living_totals(key, part):
    key = jax.random.fold_in(key, 13)
    first_key, second_key = jax.random.split(key, 2)
    drawn = jax.random.randint(first_key, (SNAPSHOT_COUNT,), SAMPLES_EACH_DAY // 2, SAMPLES_EACH_DAY + 1)
    full_at = jax.random.randint(second_key, (), 0, SNAPSHOT_COUNT)
    places = lax.broadcasted_iota(jnp.int32, (SNAPSHOT_COUNT,), 0)
    return jnp.where(places == full_at, SAMPLES_EACH_DAY, drawn).astype(jnp.int32)


def levels(own_key, dims, pieces, least, top_value):
    gain, own = 1.0, jax.random.fold_in(own_key, 6)
    for position, parts in pieces:
        steps = jnp.exp(jax.random.uniform(jax.random.fold_in(own, position), (parts,), jnp.float32, least / len(pieces), top_value / len(pieces)))
        gain = gain * jnp.repeat(steps, dims[position] // parts).reshape([-1 if axis == position else 1 for axis in range(len(dims))])
    return gain


def gaussian(key, dims, scale, reach, cuts=(), kind=jnp.bfloat16):
    values = scale * jax.random.normal(key, dims, jnp.float32)
    if cuts:
        values = values * levels(key, dims, cuts, -0.22, 0.18)
    return jnp.clip(values, -reach, reach).astype(kind)


def setup_inputs(seed: int = 0, part: int = 0) -> dict:
    keys = jax.random.split(jax.random.key(seed), 5)
    part_splits = jax.random.split(jax.random.fold_in(keys[4], part), 5)
    principal_coordinates = gaussian(part_splits[0], (SNAPSHOT_COUNT, D, SAMPLES_EACH_DAY), 1.0, 6.0, ((0, 2), (2, 8)))
    present_potentials = jnp.clip(jnp.exp(math.log(4.0) - 2.7725887 * jax.random.uniform(part_splits[1], (SNAPSHOT_COUNT, SAMPLES_EACH_DAY), jnp.float32) ** levels(part_splits[1], (SNAPSHOT_COUNT, SAMPLES_EACH_DAY), ((0, 2), (1, 8)), -0.2, 0.2)), 0.25, 4.0)
    destination_tiles = draw_destination_tiles(jax.random.fold_in(jax.random.fold_in(keys[4], part), 71), part)
    living_totals = draw_living_totals(jax.random.fold_in(jax.random.fold_in(keys[4], part), 71), part)
    return {"principal_coordinates": principal_coordinates, "present_potentials": present_potentials, "destination_tiles": destination_tiles, "living_totals": living_totals}


spread = 0.5
highest = lax.Precision.HIGHEST

def block_tiles(source, target_blocks, block_lists):
    source_f = source.astype(jnp.float32)
    chosen = target_blocks[:, block_lists].astype(jnp.float32)
    inner_prod = jnp.einsum('di,dnj->nij', source_f, chosen, precision=highest)
    source_sq = lax.optimization_barrier(jnp.sum(source_f * source_f, axis=0))
    target_sq = lax.optimization_barrier(jnp.sum(chosen * chosen, axis=0))
    distance = (source_sq[None, :, None] + target_sq[:, None, :] - 2.0 * inner_prod) / D
    return jnp.exp((2.0 - distance) / spread) / (2 * NB * BLK)

def push_forward(feats_now, feats_next, block_lists, running_belief):
    source_blocks = jnp.transpose(feats_now.reshape(D, NBLK, BLK), (1, 0, 2))
    target_blocks = feats_next.reshape(D, NBLK, BLK)

    def one_block(item):
        source, lists_here, weights = item
        kernel_tiles = block_tiles(source, target_blocks, lists_here)
        return jnp.einsum('nij,i->nj', kernel_tiles, weights, precision=highest)
    pushed = lax.map(one_block, (source_blocks, block_lists, running_belief.reshape(NBLK, BLK)))
    totals = jnp.zeros((NBLK, BLK), jnp.float32).at[block_lists.reshape(-1)].add(pushed.reshape(NBLK * NB, BLK))
    return totals.reshape(SAMPLES_EACH_DAY)

def pull_back(feats_now, feats_next, block_lists, successor_kernel):
    source_blocks = jnp.transpose(feats_now.reshape(D, NBLK, BLK), (1, 0, 2))
    target_blocks = feats_next.reshape(D, NBLK, BLK)
    later_blocks = successor_kernel.reshape(NBLK, BLK)

    def one_block(item):
        source, lists_here = item
        kernel_tiles = block_tiles(source, target_blocks, lists_here)
        picked = later_blocks[lists_here]
        return jnp.einsum('nij,nj->i', kernel_tiles, picked, precision=highest)
    pulled = lax.map(one_block, (source_blocks, block_lists))
    return pulled.reshape(SAMPLES_EACH_DAY)

def reference(principal_coordinates, present_potentials, destination_tiles, living_totals):
    positions = lax.broadcasted_iota(jnp.int32, (SNAPSHOT_COUNT, SAMPLES_EACH_DAY), 1)
    living_sample_flags = (positions < living_totals[:, None]).astype(jnp.float32)
    rightward_belief_entries = [jnp.ones((SAMPLES_EACH_DAY,), jnp.float32)]
    for present_projection in range(SNAPSHOT_COUNT - 1):
        running_belief = present_potentials[present_projection] * rightward_belief_entries[-1] * living_sample_flags[present_projection]
        rightward_belief_entries.append(push_forward(principal_coordinates[present_projection], principal_coordinates[present_projection + 1], destination_tiles[present_projection], running_belief))
    leftward_belief_entries = [jnp.ones((SAMPLES_EACH_DAY,), jnp.float32)]
    for present_projection in range(SNAPSHOT_COUNT - 2, -1, -1):
        successor_kernel = present_potentials[present_projection + 1] * leftward_belief_entries[0] * living_sample_flags[present_projection + 1]
        leftward_belief_entries.insert(0, pull_back(principal_coordinates[present_projection], principal_coordinates[present_projection + 1], destination_tiles[present_projection], successor_kernel))
    rightward_belief = jnp.stack(rightward_belief_entries)
    leftward_belief = jnp.stack(leftward_belief_entries)
    prior_projections = present_potentials * rightward_belief * leftward_belief * living_sample_flags
    wanted_density = living_sample_flags * SAMPLES_EACH_DAY / living_totals[:, None].astype(jnp.float32)
    safe_multiplied = jnp.where(living_sample_flags > 0, prior_projections, 1.0)
    renewed_potentials = jnp.where(living_sample_flags > 0, present_potentials * jnp.sqrt(wanted_density / safe_multiplied), 0.0)
    return (renewed_potentials, prior_projections)
```

```python
import functools
import math

import jax
import jax.numpy as jnp
from jax import lax
from jax.experimental import pallas as pl
from jax.experimental.pallas import tpu as pltpu
from jax.sharding import PartitionSpec as P

spread = 0.5
dead_exponent = -32768.0
vmem_bytes = 32 * 1024 * 1024


def pieces(value):
    high = value.astype(jnp.bfloat16).astype(jnp.float32)
    rest = value - high
    mid = rest.astype(jnp.bfloat16).astype(jnp.float32)
    return high, mid, (rest - mid).astype(jnp.bfloat16).astype(jnp.float32)


def stacked_rows(rows, width):
    row_ids = lax.broadcasted_iota(jnp.int32, (8, width), 0)
    block = jnp.zeros((8, width), jnp.float32)
    for place, row in enumerate(rows):
        block = jnp.where(row_ids == place, row, block)
    return block


def first_cell(row_count):
    group = lax.axis_index("cells") * lax.axis_size("feat") + lax.axis_index("feat")
    return group * row_count


def pack_kernel(offset, totals_ref, feats_ref, weights_ref, lists_ref, out_ref):
    feats = feats_ref[0]
    feat_count, row_count = feats.shape
    _, source_count, list_len = lists_ref.shape
    wide = feats.astype(jnp.float32)
    squares = jnp.sum(wide * wide, axis=0, keepdims=True)
    positions = first_cell(row_count) + lax.broadcasted_iota(jnp.int32, (1, row_count), 1)
    weights = weights_ref[...]
    used = (positions < totals_ref[lax.axis_index("tm")]) & (weights > 1e-37)
    share = offset - squares / (spread * feat_count) + jnp.log(jnp.where(used, weights, 1.0))
    high, mid, low = pieces(jnp.where(used, share, dead_exponent))
    lists = lists_ref[0].astype(jnp.float32)
    listed = jnp.concatenate(
        [lists[place : place + 1] for place in range(source_count)]
        + [jnp.full((1, row_count - source_count * list_len), -1.0, jnp.float32)],
        axis=1,
    )
    tail = stacked_rows([high, mid, low, 1.0, 1.0, 1.0, listed], row_count)
    out_ref[...] = jnp.concatenate([feats, tail.astype(jnp.bfloat16)], axis=0)


def own_kernel(feats_ref, out_ref):
    feats = feats_ref[0].astype(jnp.float32)
    feat_count, row_count = feats.shape
    squares = jnp.sum(feats * feats, axis=0, keepdims=True)
    high, mid, low = pieces(-squares / (spread * feat_count))
    tail = stacked_rows([1.0, 1.0, 1.0, high, mid, low], row_count)
    scaled = feats * (2.0 / (spread * feat_count))
    fill = jnp.zeros((out_ref.shape[1] - feat_count - 8, row_count), jnp.float32)
    columns = jnp.concatenate([scaled, tail, fill], axis=0)
    out_ref[...] = columns.T.astype(jnp.bfloat16)


def updated(alive, potentials, message):
    _, row_count = potentials.shape
    positions = first_cell(row_count) + lax.broadcasted_iota(jnp.int32, (1, row_count), 1)
    live = positions < alive
    prior = jnp.where(live, potentials * message, 0.0)
    cell_total = row_count * lax.axis_size("cells") * lax.axis_size("feat")
    wanted = cell_total / alive.astype(jnp.float32)
    scales = potentials * jnp.sqrt(wanted / jnp.where(live, prior, 1.0))
    return jnp.where(live, scales, 0.0), prior


def sum_kernel(groups, forward, closing, totals_ref, own_ref, lists_ref, weights_ref, *refs):
    shards, (scales_ref, prior_ref, acc_ref) = refs[:-3], refs[-3:]
    depth, row_count = shards[0].shape
    _, source_count, list_len = lists_ref.shape
    block_len = row_count // source_count
    time_here = lax.axis_index("tm")
    by_sender = time_here > 0 if forward is None else jnp.bool_(forward)
    here = lax.axis_index("cells") * lax.axis_size("feat") + lax.axis_index("feat")
    lists = lists_ref[0].astype(jnp.float32)
    lane = lax.broadcasted_iota(jnp.int32, (1, 128), 1)
    lister = lane // list_len
    own_lists = jnp.concatenate(
        [lists[place : place + 1] for place in range(source_count)]
        + [jnp.full((1, 128 - source_count * list_len), -1.0, jnp.float32)],
        axis=1,
    )
    acc_ref[...] = jnp.zeros_like(acc_ref)
    for shard_ref, group_of in zip(shards, groups):
        there = group_of()
        sent_lists = shard_ref[depth - 8 :, :128].astype(jnp.float32)[6:7]
        values = jnp.where(by_sender, sent_lists, own_lists)
        wanted = jnp.where(by_sender, here, there) * source_count
        mask = jnp.zeros((1, 128), jnp.int32)
        for place in range(source_count):
            bit = jnp.where(by_sender, place * source_count + lister, lister * source_count + place)
            hit = values == (wanted + place).astype(jnp.float32)
            mask = mask + jnp.where(hit, jnp.left_shift(1, bit), 0)
        pairs = jnp.sum(mask)

        def pair(index, carry, shard_ref=shard_ref, pairs=pairs):
            @pl.when(jnp.bitwise_and(jnp.right_shift(pairs, index), 1) == 1)
            def _():
                row = pl.multiple_of(index // source_count * block_len, block_len)
                column = pl.multiple_of(index % source_count * block_len, block_len)
                exponents = jnp.dot(
                    own_ref[pl.ds(row, block_len), :depth],
                    shard_ref[:, pl.ds(column, block_len)],
                    preferred_element_type=jnp.float32,
                )
                values = jnp.exp(exponents)
                total = values[:, :128]
                for start in range(128, block_len, 128):
                    total = total + values[:, start : start + 128]
                acc_ref[pl.ds(row, block_len), :] += total

            return carry

        lax.fori_loop(0, source_count * source_count, pair, 0)
    message = jnp.sum(acc_ref[...].T, axis=0, keepdims=True)
    if not closing:
        scales_ref[...] = message
        prior_ref[...] = message
        return
    scales_ref[...], prior_ref[...] = updated(totals_ref[time_here], weights_ref[...], message)


def call(kernel, out_shapes, operands, scratch=(), scalars=1):
    specs = [pl.BlockSpec(memory_space=pltpu.SMEM)] * scalars
    specs += [pl.BlockSpec(memory_space=pltpu.VMEM)] * (len(operands) - scalars)
    return pl.pallas_call(
        kernel,
        out_shape=out_shapes,
        in_specs=specs,
        out_specs=jax.tree.map(lambda _: pl.BlockSpec(memory_space=pltpu.VMEM), out_shapes),
        scratch_shapes=scratch,
        compiler_params=pltpu.CompilerParams(vmem_limit_bytes=vmem_bytes),
    )(*operands)


def collected(payload, step):
    times, count, cores = lax.axis_size("tm"), lax.axis_size("cells"), lax.axis_size("feat")
    xor = count & (count - 1) == 0

    def partner(place, distance):
        return place ^ distance if xor else (place + distance) % count

    arrived, groups = [], []
    for distance in reversed(range(count)):
        route = [
            ((time * count + place) * cores + core, ((time + move) * count + partner(place, distance)) * cores + core)
            for time in range(times)
            for move in ((1, -1) if step is None else (step,))
            if 0 <= time + move < times
            for place in range(count)
            for core in range(cores)
        ]
        shard = lax.ppermute(payload, ("tm", "cells", "feat"), route)
        for swap in range(cores):
            if swap:
                twin = [(core, (core + swap) % cores) for core in range(cores)]
                shard_here = lax.ppermute(shard, "feat", twin)
            else:
                shard_here = shard

            def group_of(distance=distance, swap=swap):
                place, core = lax.axis_index("cells"), lax.axis_index("feat")
                if xor:
                    source = jnp.bitwise_xor(place, distance)
                else:
                    source = lax.rem(place + count - distance, count)
                return source * cores + lax.rem(core + cores - swap, cores)

            arrived.append(shard_here)
            groups.append(group_of)
    return arrived, groups


def on_device(principal_coordinates, present_potentials, destination_tiles, living_totals):
    _, feat_count, row_count = principal_coordinates.shape
    _, source_count, list_len = destination_tiles.shape
    block_len = row_count // source_count
    offset = 2.0 / spread - math.log(2 * list_len * block_len)
    row = jax.ShapeDtypeStruct((1, row_count), jnp.float32)
    payload_shape = jax.ShapeDtypeStruct((feat_count + 8, row_count), jnp.bfloat16)
    own_shape = jax.ShapeDtypeStruct((row_count, 128), jnp.bfloat16)
    scratch = [pltpu.VMEM((row_count, 128), jnp.float32)]
    times = lax.axis_size("tm")

    def packed(weights):
        operands = (living_totals, principal_coordinates, weights, destination_tiles)
        return call(functools.partial(pack_kernel, offset), payload_shape, operands)

    def summed(payload, step, weights):
        arrived, groups = collected(payload, step)
        forward = None if step is None else step > 0
        operands = (living_totals, own_cells, destination_tiles, weights, *arrived)
        kernel = functools.partial(sum_kernel, groups, forward, step is None)
        return call(kernel, (row, row), operands, scratch)

    own_cells = call(own_kernel, own_shape, (principal_coordinates,), scalars=0)
    if times == 2:
        return tuple(summed(packed(present_potentials), None, present_potentials))

    time_here = lax.axis_index("tm")

    def advance(_, state):
        forward, backward = state
        pushed, _ = summed(packed(present_potentials * forward), 1, present_potentials)
        pulled, _ = summed(packed(present_potentials * backward), -1, present_potentials)
        return (
            jnp.where(time_here == 0, 1.0, pushed),
            jnp.where(time_here == times - 1, 1.0, pulled),
        )

    unit = jnp.ones((1, row_count), jnp.float32)
    forward, backward = lax.fori_loop(0, times - 1, advance, (unit, unit))
    return updated(living_totals[time_here], present_potentials, forward * backward)


def solution(mesh):
    in_specs = (
        P(("runs", "tm"), None, ("cells", "feat")),
        P(("runs", "tm"), ("cells", "feat")),
        P(("runs", "tm"), ("cells", "feat"), None),
        P("runs"),
    )
    out_specs = (P(("runs", "tm"), ("cells", "feat")), P(("runs", "tm"), ("cells", "feat")))
    return jax.shard_map(
        on_device, mesh=mesh, in_specs=in_specs, out_specs=out_specs, check_vma=False
    )
```

```python
import functools
import math

import jax
import jax.numpy as jnp
from jax import lax
from jax.experimental import pallas as pl
from jax.experimental.pallas import tpu as pltpu
from jax.sharding import PartitionSpec as P

spread = 0.5
dead_exponent = -32768.0
vmem_bytes = 32 * 1024 * 1024
lanes = 128
extra_rows = 32
list_rows = 16
bf16 = jnp.bfloat16


def pieces(value):
    high = value.astype(bf16).astype(jnp.float32)
    rest = value - high
    mid = rest.astype(bf16).astype(jnp.float32)
    return high, mid, (rest - mid).astype(bf16).astype(jnp.float32)


def stacked_rows(rows, height, width):
    row_ids = lax.broadcasted_iota(jnp.int32, (height, width), 0)
    block = jnp.zeros((height, width), jnp.float32)
    for place, row in enumerate(rows):
        block = jnp.where(row_ids == place, row, block)
    return block


def lane_blocks(row):
    return jnp.concatenate(
        [row[:, start : start + lanes] for start in range(0, row.shape[1], lanes)], axis=0
    )


def here():
    return lax.axis_index("cells") * lax.axis_size("feat") + lax.axis_index("feat")


def listed_row(lists):
    source_count, list_len = lists.shape
    rows = [lists[place : place + 1] for place in range(source_count)]
    fill = jnp.full((1, lanes - source_count * list_len), -1.0, jnp.float32)
    return jnp.concatenate(rows + [fill], axis=1)


def fetch(sources, targets, sems):
    copies = [
        pltpu.make_async_copy(source, target, sems.at[place])
        for place, (source, target) in enumerate(zip(sources, targets))
    ]
    for copy in copies:
        copy.start()
    for copy in copies:
        copy.wait()


def pack_kernel(
    offset, totals_hbm, feats_hbm, weights_hbm, lists_hbm, out_ref, own_ref, facts_ref, *scratch
):
    totals_ref, feats_ref, weights_ref, lists_ref, sems = scratch
    fetch((feats_hbm, weights_hbm, lists_hbm, totals_hbm), (feats_ref, weights_ref, lists_ref, totals_ref), sems)
    _, feat_count, row_count = feats_ref.shape
    _, source_count, _ = lists_ref.shape
    slabs = row_count // lanes
    feats = feats_ref[0]
    wide = feats.astype(jnp.float32)
    squares = jnp.sum(wide * wide, axis=0, keepdims=True) / (spread * feat_count)
    positions = here() * row_count + lax.broadcasted_iota(jnp.int32, (1, row_count), 1)
    weights = weights_ref[...]
    alive = totals_ref[lax.axis_index("tm")]
    used = (positions < alive) & (weights > 1e-37)
    share = offset - squares + jnp.log(jnp.where(used, weights, 1.0))
    share = lane_blocks(jnp.where(used, share, dead_exponent))
    listed = listed_row(lists_ref[0].astype(jnp.float32))
    fill = jnp.zeros((extra_rows - 3 * slabs, lanes), jnp.float32)
    tail = jnp.concatenate([*pieces(share), fill + listed], axis=0)
    for slab in range(slabs):
        out_ref[slab * feat_count : (slab + 1) * feat_count, :] = feats[:, slab * lanes : (slab + 1) * lanes]
    out_ref[slabs * feat_count :, :] = tail.astype(bf16)
    block = lax.broadcasted_iota(jnp.int32, (1, row_count), 1) // (row_count // source_count)
    cores = lax.axis_size("feat")
    block = block + lax.axis_index("feat") * source_count
    member = [jnp.where(block == place, 1.0, 0.0) for place in range(cores * source_count)]
    own_tail = stacked_rows(
        [1.0, 1.0, 1.0, *pieces(-squares), *member], own_ref.shape[1] - feat_count, row_count
    )
    columns = jnp.concatenate([wide * (2.0 / (spread * feat_count)), own_tail], axis=0)
    own_ref[:row_count, :] = columns.T.astype(bf16)
    own_ref[row_count:, :] = jnp.broadcast_to(listed, (list_rows, lanes)).astype(bf16)
    facts_ref[...] = stacked_rows([weights, alive.astype(jnp.float32)], 8, row_count)


def updated(alive, potentials, message):
    _, row_count = potentials.shape
    positions = here() * row_count + lax.broadcasted_iota(jnp.int32, (1, row_count), 1)
    live = positions.astype(jnp.float32) < alive
    prior = jnp.where(live, potentials * message, 0.0)
    cell_total = row_count * lax.axis_size("cells") * lax.axis_size("feat")
    wanted = cell_total / alive
    scales = potentials * jnp.sqrt(wanted / jnp.where(live, prior, 1.0))
    return jnp.where(live, scales, 0.0), prior


def listed_pairs(values, first, by_sender, list_shape):
    source_count, list_len = list_shape
    lister = lax.broadcasted_iota(jnp.int32, (1, lanes), 1) // list_len
    found = jnp.zeros((1, lanes), jnp.int32)
    for place in range(source_count):
        bit = jnp.where(by_sender, place * source_count + lister, lister * source_count + place)
        hit = values == (first + place).astype(jnp.float32)
        found = found + jnp.where(hit, jnp.left_shift(1, bit), 0)
    return jnp.sum(found)


def add_shard(shard_ref, there, forward, list_shape, owners, totals):
    source_count, _ = list_shape
    cores = lax.axis_size("feat")
    row_count = owners[0][0].shape[0] - list_rows
    slabs = row_count // lanes
    feat_count = (shard_ref.shape[0] - extra_rows) // slabs
    depth = feat_count + 16
    by_sender = lax.axis_index("tm") > 0 if forward is None else jnp.bool_(forward)
    tail = shard_ref[slabs * feat_count :, :].astype(jnp.float32)
    pairs = []
    for own_ref, core in owners:
        lists = own_ref[row_count:, :].astype(jnp.float32)[:1]
        values = jnp.where(by_sender, tail[3 * slabs : 3 * slabs + 1], lists)
        group = lax.axis_index("cells") * cores + core
        first = jnp.where(by_sender, group, there) * source_count
        pairs.append((listed_pairs(values, first, by_sender, list_shape), core))
    cells = [own_ref[:row_count, :depth] for own_ref, _ in owners]
    cells = jnp.concatenate(cells, axis=0) if len(owners) > 1 else cells[0]
    for start in range(0, slabs, 2):
        other = start * source_count // slabs
        shut = []
        for core in range(cores):
            open_here = sum(jnp.where(owner == core, bits, 0) for bits, owner in pairs)
            for place in range(source_count):
                bit = jnp.bitwise_and(jnp.right_shift(open_here, place * source_count + other), 1)
                shut.append(jnp.where(bit == 1, 0.0, dead_exponent))
        columns = []
        for slab in (start, start + 1):
            share = [tail[piece * slabs + slab : piece * slabs + slab + 1] for piece in range(3)]
            rows = stacked_rows([*share, 1.0, 1.0, 1.0, *shut], 16, lanes).astype(bf16)
            feats = shard_ref[slab * feat_count : (slab + 1) * feat_count, :]
            columns.append(jnp.concatenate([feats, rows], axis=0))
        exponents = jnp.dot(
            cells, jnp.concatenate(columns, axis=1), preferred_element_type=jnp.float32
        )
        terms = jnp.exp(exponents)
        terms = terms[:, :lanes] + terms[:, lanes:]
        totals = [
            total + terms[place * row_count : (place + 1) * row_count]
            for place, total in enumerate(totals)
        ]
    return totals


def across(total):
    return jnp.sum(total.T, axis=0, keepdims=True)


def chip_kernel(groups, forward, list_shape, opening, closing, *refs):
    cores = lax.axis_size("feat")
    shards = refs[: len(groups)]
    own_refs = refs[len(groups) : len(groups) + cores]
    refs = refs[len(groups) + cores :]
    core = lax.axis_index("feat")
    owners = [
        (own_ref, lax.rem(core + cores - swap, cores)) for swap, own_ref in enumerate(own_refs)
    ]
    totals = [jnp.zeros((own_refs[0].shape[0] - list_rows, lanes), jnp.float32)] * cores
    if not opening:
        totals, refs = [total_ref[...] for total_ref in refs[:cores]], refs[cores:]
    for shard_ref, group_of in zip(shards, groups):
        totals = add_shard(shard_ref, group_of(), forward, list_shape, owners, totals)
    for out_ref, total in zip(refs, totals):
        out_ref[...] = across(total) if closing else total


def last_kernel(group_of, forward, list_shape, opening, partials, shard_ref, own_ref, *refs):
    total = jnp.zeros((own_ref.shape[0] - list_rows, lanes), jnp.float32)
    if not opening:
        total, refs = refs[0][...], refs[1:]
    owners = [(own_ref, lax.axis_index("feat"))]
    (total,) = add_shard(shard_ref, group_of(), forward, list_shape, owners, [total])
    if partials is None:
        refs[0][...] = total
        return
    message = across(total)
    for partial_ref in refs[:partials]:
        message = message + partial_ref[...]
    refs = refs[partials:]
    if forward is not None:
        refs[0][...] = message
        return
    facts_ref, scales_ref, prior_ref = refs
    scales_ref[...], prior_ref[...] = updated(facts_ref[1:2], facts_ref[0:1], message)


def call(kernel, name, out_shapes, operands, spaces=None, scratch=(), exps=0):
    spaces = spaces or [pltpu.VMEM] * len(operands)
    return pl.pallas_call(
        kernel,
        name=name,
        out_shape=out_shapes,
        in_specs=[pl.BlockSpec(memory_space=space) for space in spaces],
        out_specs=jax.tree.map(lambda _: pl.BlockSpec(memory_space=pltpu.VMEM), out_shapes),
        scratch_shapes=scratch,
        compiler_params=pltpu.CompilerParams(vmem_limit_bytes=vmem_bytes),
        cost_estimate=pl.CostEstimate(flops=160 * exps, bytes_accessed=2**17, transcendentals=exps),
    )(*operands)


def exchange(array, route):
    (moves, shift) = route
    times, count, cores = lax.axis_size("tm"), lax.axis_size("cells"), lax.axis_size("feat")
    pairs = [
        ((time * count + place) * cores + core, ((time + move) * count + shift(place)) * cores + core)
        for time in range(times)
        for move in moves
        if 0 <= time + move < times
        for place in range(count)
        for core in range(cores)
    ]
    return lax.ppermute(array, ("tm", "cells", "feat"), pairs)


def swapped(array, swap):
    cores = lax.axis_size("feat")
    return lax.ppermute(array, "feat", [(core, (core + swap) % cores) for core in range(cores)])


def collected(payload, step):
    count, cores = lax.axis_size("cells"), lax.axis_size("feat")
    moves = (1, -1) if step is None else (step,)
    xor = count & (count - 1) == 0 and count > 1

    def shifted(distance):
        return lambda place: place ^ distance if xor else (place + distance) % count

    def group_of(distance, swap):
        place, core = lax.axis_index("cells"), lax.axis_index("feat")
        source = jnp.bitwise_xor(place, distance) if xor else lax.rem(place + count - distance, count)
        return source * cores + lax.rem(core + cores - swap, cores)

    direct = [d for d in reversed(range(count)) if not xor or d % 2 == 0 or d == 1]
    direct = sorted(direct, key=lambda d: d < 2)
    shards = {d: exchange(payload, (moves, shifted(d))) for d in direct}
    order = sorted(direct, key=lambda d: d >= 2)
    for distance in range(count):
        if distance not in shards:
            shards[distance] = exchange(shards[distance - 1], ((0,), shifted(1)))
            order.append(distance)
    return [(shards[distance], functools.partial(group_of, distance)) for distance in order]


def on_device(principal_coordinates, present_potentials, destination_tiles, living_totals):
    _, feat_count, row_count = principal_coordinates.shape
    _, source_count, list_len = destination_tiles.shape
    block_len = row_count // source_count
    offset = 2.0 / spread - math.log(2 * list_len * block_len)
    times = lax.axis_size("tm")
    row = jax.ShapeDtypeStruct((1, row_count), jnp.float32)
    sums = jax.ShapeDtypeStruct((row_count, lanes), jnp.float32)
    payload_rows = feat_count * row_count // lanes + extra_rows
    smem, vmem = pltpu.SMEM, pltpu.VMEM

    scratch = [
        smem(living_totals.shape, jnp.int32),
        vmem(principal_coordinates.shape, bf16),
        vmem(present_potentials.shape, jnp.float32),
        vmem(destination_tiles.shape, jnp.int32),
        pltpu.SemaphoreType.DMA((4,)),
    ]

    def in_hbm(*arrays):
        return [pltpu.with_memory_space_constraint(array, pltpu.HBM) for array in arrays]

    def packed(weights):
        return call(
            functools.partial(pack_kernel, offset),
            "pack_cells",
            (
                jax.ShapeDtypeStruct((payload_rows, lanes), bf16),
                jax.ShapeDtypeStruct((row_count + list_rows, lanes), bf16),
                jax.ShapeDtypeStruct((8, row_count), jnp.float32),
            ),
            in_hbm(living_totals, principal_coordinates, weights, destination_tiles),
            [pltpu.HBM] * 4,
            scratch,
        )

    def summed(pack, step):
        payload, own, facts = pack
        cores = lax.axis_size("feat")
        list_shape = (source_count, list_len)
        forward = None if step is None else step > 0
        owns = [own] + [swapped(own, swap) for swap in range(1, cores)]
        *early, (last, last_group) = collected(payload, step)
        rows = []
        batches = [early[2:], early[:1], early[1:2]] if len(early) > 2 else [early]
        for place, batch in enumerate(batches):
            closing = place == len(batches) - 1
            rows = call(
                functools.partial(
                    chip_kernel,
                    [functools.partial(group_of, 0) for _, group_of in batch],
                    forward,
                    list_shape,
                    place == 0,
                    closing,
                ),
                "chip_sums",
                (row if closing else sums,) * cores,
                [*(shard for shard, _ in batch), *owns, *rows],
                exps=len(batch) * cores * row_count * row_count,
            )
        partials = [rows[0]] + [swapped(rows[swap], cores - swap) for swap in range(1, cores)]
        last, _ = lax.optimization_barrier((last, rows[0]))
        total = []
        for swap in range(cores):
            shard = swapped(last, swap) if swap else last
            closing = swap == cores - 1
            operands = [shard, own, *total]
            result = sums
            if closing:
                operands += partials
                result = row
                if step is None:
                    operands.append(facts)
                    result = (row, row)
            total = call(
                functools.partial(
                    last_kernel,
                    functools.partial(last_group, swap),
                    forward,
                    list_shape,
                    swap == 0,
                    len(partials) if closing else None,
                ),
                "last_sums",
                result,
                operands,
                exps=row_count * row_count,
            )
            if not closing:
                total = [total]
        return total

    if times == 2:
        return tuple(summed(packed(present_potentials), None))

    time_here = lax.axis_index("tm")

    def advance(_, state):
        forward, backward = state
        pushed = summed(packed(present_potentials * forward), 1)
        pulled = summed(packed(present_potentials * backward), -1)
        return (
            jnp.where(time_here == 0, 1.0, pushed),
            jnp.where(time_here == times - 1, 1.0, pulled),
        )

    unit = jnp.ones((1, row_count), jnp.float32)
    forward, backward = lax.fori_loop(0, times - 1, advance, (unit, unit))
    return updated(living_totals[time_here].astype(jnp.float32), present_potentials, forward * backward)


def solution(mesh):
    in_specs = (
        P(("runs", "tm"), None, ("cells", "feat")),
        P(("runs", "tm"), ("cells", "feat")),
        P(("runs", "tm"), ("cells", "feat"), None),
        P("runs"),
    )
    out_specs = (P(("runs", "tm"), ("cells", "feat")), P(("runs", "tm"), ("cells", "feat")))
    return jax.shard_map(
        on_device, mesh=mesh, in_specs=in_specs, out_specs=out_specs, check_vma=False
    )
```

```python
import functools
import math

import jax
import jax.numpy as jnp
from jax import lax
from jax.experimental import pallas as pl
from jax.experimental.pallas import tpu as pltpu
from jax.sharding import PartitionSpec as P

spread = 0.5
dead_exponent = -32768.0
vmem_bytes = 32 * 1024 * 1024
lanes = 128
extra_rows = 32
list_rows = 16
bf16 = jnp.bfloat16


def pieces(value):
    high = value.astype(bf16).astype(jnp.float32)
    rest = value - high
    mid = rest.astype(bf16).astype(jnp.float32)
    return high, mid, (rest - mid).astype(bf16).astype(jnp.float32)


def stacked_rows(rows, height, width):
    row_ids = lax.broadcasted_iota(jnp.int32, (height, width), 0)
    block = jnp.zeros((height, width), jnp.float32)
    for place, row in enumerate(rows):
        block = jnp.where(row_ids == place, row, block)
    return block


def lane_blocks(row):
    return jnp.concatenate(
        [row[:, start : start + lanes] for start in range(0, row.shape[1], lanes)], axis=0
    )


def here():
    return lax.axis_index("cells") * lax.axis_size("feat") + lax.axis_index("feat")


def listed_row(lists):
    source_count, list_len = lists.shape
    rows = [lists[place : place + 1] for place in range(source_count)]
    fill = jnp.full((1, lanes - source_count * list_len), -1.0, jnp.float32)
    return jnp.concatenate(rows + [fill], axis=1)


def fetch(sources, targets, sems):
    copies = [
        pltpu.make_async_copy(source, target, sems.at[place])
        for place, (source, target) in enumerate(zip(sources, targets))
    ]
    for copy in copies:
        copy.start()
    for copy in copies:
        copy.wait()


def pack_kernel(
    offset, totals_hbm, feats_hbm, weights_hbm, lists_hbm, out_ref, facts_ref, *scratch
):
    totals_ref, feats_ref, weights_ref, lists_ref, sems = scratch
    fetch((feats_hbm, weights_hbm, lists_hbm, totals_hbm), (feats_ref, weights_ref, lists_ref, totals_ref), sems)
    _, feat_count, row_count = feats_ref.shape
    _, source_count, _ = lists_ref.shape
    slabs = row_count // lanes
    feats = feats_ref[0]
    wide = feats.astype(jnp.float32)
    squares = jnp.sum(wide * wide, axis=0, keepdims=True) / (spread * feat_count)
    positions = here() * row_count + lax.broadcasted_iota(jnp.int32, (1, row_count), 1)
    weights = weights_ref[...]
    alive = totals_ref[lax.axis_index("tm")]
    used = (positions < alive) & (weights > 1e-37)
    share = offset - squares + jnp.log(jnp.where(used, weights, 1.0))
    share = lane_blocks(jnp.where(used, share, dead_exponent))
    listed = listed_row(lists_ref[0].astype(jnp.float32))
    fill = jnp.zeros((extra_rows - 3 * slabs, lanes), jnp.float32)
    tail = jnp.concatenate([*pieces(share), fill + listed], axis=0)
    for slab in range(slabs):
        out_ref[slab * feat_count : (slab + 1) * feat_count, :] = feats[:, slab * lanes : (slab + 1) * lanes]
    out_ref[slabs * feat_count :, :] = tail.astype(bf16)
    facts_ref[...] = stacked_rows([weights, alive.astype(jnp.float32)], 8, row_count)


def own_kernel(source_count, payload_ref, own_ref):
    row_count = own_ref.shape[0] - list_rows
    slabs = row_count // lanes
    feat_count = (payload_ref.shape[0] - extra_rows) // slabs
    feats = [payload_ref[slab * feat_count : (slab + 1) * feat_count, :] for slab in range(slabs)]
    wide = jnp.concatenate(feats, axis=1).astype(jnp.float32)
    squares = jnp.sum(wide * wide, axis=0, keepdims=True) / (spread * feat_count)
    cores = lax.axis_size("feat")
    block = lax.broadcasted_iota(jnp.int32, (1, row_count), 1) // (row_count // source_count)
    block = block + lax.axis_index("feat") * source_count
    member = [jnp.where(block == place, 1.0, 0.0) for place in range(cores * source_count)]
    own_tail = stacked_rows(
        [1.0, 1.0, 1.0, *pieces(-squares), 0.0, 0.0, *member], lanes - feat_count, row_count
    )
    columns = jnp.concatenate([wide * (2.0 / (spread * feat_count)), own_tail], axis=0)
    own_ref[:row_count, :] = columns.T.astype(bf16)
    tail = payload_ref[slabs * feat_count :, :].astype(jnp.float32)
    listed = tail[3 * slabs : 3 * slabs + 1]
    own_ref[row_count:, :] = jnp.broadcast_to(listed, (list_rows, lanes)).astype(bf16)


def updated(alive, potentials, message):
    _, row_count = potentials.shape
    positions = here() * row_count + lax.broadcasted_iota(jnp.int32, (1, row_count), 1)
    live = positions.astype(jnp.float32) < alive
    prior = jnp.where(live, potentials * message, 0.0)
    cell_total = row_count * lax.axis_size("cells") * lax.axis_size("feat")
    wanted = cell_total / alive
    scales = potentials * jnp.sqrt(wanted / jnp.where(live, prior, 1.0))
    return jnp.where(live, scales, 0.0), prior


def closed_pairs(sent, lists, there, forward, list_shape):
    source_count, list_len = list_shape
    cores = lax.axis_size("feat")
    by_sender = lax.axis_index("tm") > 0 if forward is None else jnp.bool_(forward)
    shape = (source_count * 8, lanes)
    row_ids = lax.broadcasted_iota(jnp.int32, shape, 0)
    other, owner = row_ids // 8, row_ids % 8
    core, block = owner // source_count, owner % source_count
    lister = lax.broadcasted_iota(jnp.int32, shape, 1) // list_len
    values = jnp.broadcast_to(sent, shape)
    for place, own_lists in lists:
        values = jnp.where((core == place) & jnp.logical_not(by_sender), own_lists, values)
    group = lax.axis_index("cells") * cores + core
    wanted = jnp.where(by_sender, group * source_count + block, there * source_count + other)
    hit = (values == wanted.astype(jnp.float32)) & (lister == jnp.where(by_sender, other, block))
    found = jnp.max(jnp.where(hit, 1.0, 0.0), axis=1, keepdims=True)
    return jnp.broadcast_to(jnp.where(found > 0.0, 0.0, dead_exponent), shape)


def add_shard(shard_ref, there, forward, list_shape, owners, totals):
    source_count, _ = list_shape
    row_count = owners[0][0].shape[0] - list_rows
    slabs = row_count // lanes
    feat_count = (shard_ref.shape[0] - extra_rows) // slabs
    depth = feat_count + 16
    tail = shard_ref[slabs * feat_count :, :].astype(jnp.float32)
    lists = [(core, own_ref[row_count:, :].astype(jnp.float32)[:1]) for own_ref, core in owners]
    closed = closed_pairs(tail[3 * slabs : 3 * slabs + 1], lists, there, forward, list_shape)
    cells = [own_ref[:row_count, :depth] for own_ref, _ in owners]
    cells = jnp.concatenate(cells, axis=0) if len(owners) > 1 else cells[0]
    for start in range(0, slabs, 2):
        other = start * source_count // slabs
        columns = []
        for slab in (start, start + 1):
            share = [tail[piece * slabs + slab : piece * slabs + slab + 1] for piece in range(3)]
            rows = [stacked_rows([*share, 1.0, 1.0, 1.0], 8, lanes), closed[other * 8 : other * 8 + 8]]
            feats = shard_ref[slab * feat_count : (slab + 1) * feat_count, :]
            columns.append(jnp.concatenate([feats, jnp.concatenate(rows, axis=0).astype(bf16)], axis=0))
        exponents = jnp.dot(
            cells, jnp.concatenate(columns, axis=1), preferred_element_type=jnp.float32
        )
        terms = jnp.exp(exponents)
        terms = terms[:, :lanes] + terms[:, lanes:]
        totals = [
            total + terms[place * row_count : (place + 1) * row_count]
            for place, total in enumerate(totals)
        ]
    return totals


def across(total):
    return jnp.sum(total.T, axis=0, keepdims=True)


def chip_kernel(groups, jobs, forward, list_shape, started, finished, *refs):
    cores = lax.axis_size("feat")
    owner_count = 1 + max(max(swaps) for _, swaps in jobs)
    shards, refs = refs[: len(groups)], refs[len(groups) :]
    own_refs, refs = refs[:owner_count], refs[owner_count:]
    core = lax.axis_index("feat")
    owners = [
        (own_ref, lax.rem(core + cores - swap, cores)) for swap, own_ref in enumerate(own_refs)
    ]
    row_count = own_refs[0].shape[0] - list_rows
    totals = [total_ref[...] for total_ref in refs[:started]]
    totals += [jnp.zeros((row_count, lanes), jnp.float32)] * (owner_count - started)
    refs = refs[started:]
    for place, swaps in jobs:
        added = add_shard(
            shards[place],
            groups[place](),
            forward,
            list_shape,
            [owners[swap] for swap in swaps],
            [totals[swap] for swap in swaps],
        )
        for swap, total in zip(swaps, added):
            totals[swap] = total
    for swap, (out_ref, total) in enumerate(zip(refs, totals)):
        out_ref[...] = across(total) if finished and swap else total


def last_kernel(group_of, forward, list_shape, partials, shard_ref, own_ref, total_ref, *refs):
    owners = [(own_ref, lax.axis_index("feat"))]
    (total,) = add_shard(shard_ref, group_of(), forward, list_shape, owners, [total_ref[...]])
    if partials is None:
        refs[0][...] = total
        return
    message = across(total)
    for partial_ref in refs[:partials]:
        message = message + partial_ref[...]
    refs = refs[partials:]
    if forward is not None:
        refs[0][...] = message
        return
    facts_ref, scales_ref, prior_ref = refs
    scales_ref[...], prior_ref[...] = updated(facts_ref[1:2], facts_ref[0:1], message)


def call(kernel, name, out_shapes, operands, spaces=None, scratch=(), exps=0):
    spaces = spaces or [pltpu.VMEM] * len(operands)
    return pl.pallas_call(
        kernel,
        name=name,
        out_shape=out_shapes,
        in_specs=[pl.BlockSpec(memory_space=space) for space in spaces],
        out_specs=jax.tree.map(lambda _: pl.BlockSpec(memory_space=pltpu.VMEM), out_shapes),
        scratch_shapes=scratch,
        compiler_params=pltpu.CompilerParams(vmem_limit_bytes=vmem_bytes),
        cost_estimate=pl.CostEstimate(flops=160 * exps, bytes_accessed=2**17, transcendentals=exps),
    )(*operands)


def exchange(array, route):
    (moves, shift) = route
    times, count, cores = lax.axis_size("tm"), lax.axis_size("cells"), lax.axis_size("feat")
    pairs = [
        ((time * count + place) * cores + core, ((time + move) * count + shift(place)) * cores + core)
        for time in range(times)
        for move in moves
        if 0 <= time + move < times
        for place in range(count)
        for core in range(cores)
    ]
    return lax.ppermute(array, ("tm", "cells", "feat"), pairs)


def swapped(array, swap):
    cores = lax.axis_size("feat")
    return lax.ppermute(array, "feat", [(core, (core + swap) % cores) for core in range(cores)])


def collected(payload, step):
    count, cores = lax.axis_size("cells"), lax.axis_size("feat")
    moves = (1, -1) if step is None else (step,)
    xor = count & (count - 1) == 0 and count > 1

    def shifted(distance):
        return lambda place: place ^ distance if xor else (place + distance) % count

    def group_of(distance, swap):
        place, core = lax.axis_index("cells"), lax.axis_index("feat")
        source = jnp.bitwise_xor(place, distance) if xor else lax.rem(place + count - distance, count)
        return source * cores + lax.rem(core + cores - swap, cores)

    direct = [d for d in reversed(range(count)) if not xor or d % 2 == 0 or d == 1]
    direct = sorted(direct, key=lambda d: d < 2)
    shards = {d: exchange(payload, (moves, shifted(d))) for d in direct}
    order = sorted(direct, key=lambda d: d >= 2)
    for distance in range(count):
        if distance not in shards:
            shards[distance] = exchange(shards[distance - 1], ((0,), shifted(1)))
            order.append(distance)
    return [(shards[distance], functools.partial(group_of, distance)) for distance in order]


def on_device(principal_coordinates, present_potentials, destination_tiles, living_totals):
    _, feat_count, row_count = principal_coordinates.shape
    _, source_count, list_len = destination_tiles.shape
    block_len = row_count // source_count
    offset = 2.0 / spread - math.log(2 * list_len * block_len)
    times = lax.axis_size("tm")
    row = jax.ShapeDtypeStruct((1, row_count), jnp.float32)
    sums = jax.ShapeDtypeStruct((row_count, lanes), jnp.float32)
    payload_rows = feat_count * row_count // lanes + extra_rows
    smem, vmem = pltpu.SMEM, pltpu.VMEM

    scratch = [
        smem(living_totals.shape, jnp.int32),
        vmem(principal_coordinates.shape, bf16),
        vmem(present_potentials.shape, jnp.float32),
        vmem(destination_tiles.shape, jnp.int32),
        pltpu.SemaphoreType.DMA((4,)),
    ]

    def in_hbm(*arrays):
        return [pltpu.with_memory_space_constraint(array, pltpu.HBM) for array in arrays]

    def packed(weights):
        return call(
            functools.partial(pack_kernel, offset),
            "pack_cells",
            (
                jax.ShapeDtypeStruct((payload_rows, lanes), bf16),
                jax.ShapeDtypeStruct((8, row_count), jnp.float32),
            ),
            in_hbm(living_totals, principal_coordinates, weights, destination_tiles),
            [pltpu.HBM] * 4,
            scratch,
        )

    def summed(pack, step):
        payload, facts = pack
        own = call(
            functools.partial(own_kernel, source_count),
            "own_rows",
            jax.ShapeDtypeStruct((row_count + list_rows, lanes), bf16),
            (payload,),
        )
        cores = lax.axis_size("feat")
        list_shape = (source_count, list_len)
        forward = None if step is None else step > 0
        owns = [own] + [swapped(own, swap) for swap in range(1, cores)]
        *early, (last, last_group) = collected(payload, step)
        mine, everyone, others = (0,), tuple(range(cores)), tuple(range(1, cores))
        if len(early) > 2:
            first = [(shard, mine) for shard in early[2:]]
            second = [(shard, others) for shard in early[2:]]
            batches = [first, [(early[0], everyone), *second], [(early[1], everyone)]]
        else:
            batches = [[(shard, everyone) for shard in early]]
        totals = []
        for place, batch in enumerate(batches):
            finished = place == len(batches) - 1
            owner_count = 1 + max(max(swaps) for _, swaps in batch)
            totals = call(
                functools.partial(
                    chip_kernel,
                    [functools.partial(group_of, 0) for (_, group_of), _ in batch],
                    [(job, swaps) for job, (_, swaps) in enumerate(batch)],
                    forward,
                    list_shape,
                    len(totals),
                    finished,
                ),
                "chip_sums",
                tuple(row if finished and swap else sums for swap in range(owner_count)),
                [*(shard for (shard, _), _ in batch), *owns[:owner_count], *totals],
                exps=row_count * row_count * sum(len(swaps) for _, swaps in batch),
            )
        partials = [swapped(totals[swap], cores - swap) for swap in range(1, cores)]
        last, _ = lax.optimization_barrier((last, totals[0]))
        total = totals[0]
        for swap in range(cores):
            shard = swapped(last, swap) if swap else last
            closing = swap == cores - 1
            operands = [shard, own, total]
            result = sums
            if closing:
                operands += partials
                result = row
                if step is None:
                    operands.append(facts)
                    result = (row, row)
            total = call(
                functools.partial(
                    last_kernel,
                    functools.partial(last_group, swap),
                    forward,
                    list_shape,
                    len(partials) if closing else None,
                ),
                "last_sums",
                result,
                operands,
                exps=row_count * row_count,
            )
        return total

    if times == 2:
        return tuple(summed(packed(present_potentials), None))

    time_here = lax.axis_index("tm")

    def advance(_, state):
        forward, backward = state
        pushed = summed(packed(present_potentials * forward), 1)
        pulled = summed(packed(present_potentials * backward), -1)
        return (
            jnp.where(time_here == 0, 1.0, pushed),
            jnp.where(time_here == times - 1, 1.0, pulled),
        )

    unit = jnp.ones((1, row_count), jnp.float32)
    forward, backward = lax.fori_loop(0, times - 1, advance, (unit, unit))
    return updated(living_totals[time_here].astype(jnp.float32), present_potentials, forward * backward)


def solution(mesh):
    in_specs = (
        P(("runs", "tm"), None, ("cells", "feat")),
        P(("runs", "tm"), ("cells", "feat")),
        P(("runs", "tm"), ("cells", "feat"), None),
        P("runs"),
    )
    out_specs = (P(("runs", "tm"), ("cells", "feat")), P(("runs", "tm"), ("cells", "feat")))
    return jax.shard_map(
        on_device, mesh=mesh, in_specs=in_specs, out_specs=out_specs, check_vma=False
    )
```

```python
import functools
import math

import jax
import jax.numpy as jnp
from jax import lax
from jax.experimental import pallas as pl
from jax.experimental.pallas import tpu as pltpu
from jax.sharding import PartitionSpec as P

spread = 0.5
dead_exponent = -32768.0
vmem_bytes = 32 * 1024 * 1024
lanes = 128
list_rows = 16
bf16 = jnp.bfloat16


def pieces(value):
    high = value.astype(bf16).astype(jnp.float32)
    rest = value - high
    mid = rest.astype(bf16).astype(jnp.float32)
    return high, mid, (rest - mid).astype(bf16).astype(jnp.float32)


def stacked_rows(rows, height, width):
    row_ids = lax.broadcasted_iota(jnp.int32, (height, width), 0)
    block = jnp.zeros((height, width), jnp.float32)
    for place, row in enumerate(rows):
        block = jnp.where(row_ids == place, row, block)
    return block


def lane_blocks(row):
    return jnp.concatenate(
        [row[:, start : start + lanes] for start in range(0, row.shape[1], lanes)], axis=0
    )


def here():
    return lax.axis_index("cells") * lax.axis_size("feat") + lax.axis_index("feat")


def listed_row(lists):
    source_count, list_len = lists.shape
    rows = [lists[place : place + 1] for place in range(source_count)]
    fill = jnp.full((1, lanes - source_count * list_len), -1.0, jnp.float32)
    return jnp.concatenate(rows + [fill], axis=1)


def fetch(sources, targets, sems):
    copies = [
        pltpu.make_async_copy(source, target, sems.at[place])
        for place, (source, target) in enumerate(zip(sources, targets))
    ]
    for copy in copies:
        copy.start()
    for copy in copies:
        copy.wait()


def pack_kernel(
    offset, totals_hbm, feats_hbm, weights_hbm, lists_hbm, whole_ref, facts_ref, *scratch
):
    totals_ref, feats_ref, weights_ref, lists_ref, sems = scratch
    fetch((feats_hbm, weights_hbm, lists_hbm, totals_hbm), (feats_ref, weights_ref, lists_ref, totals_ref), sems)
    _, feat_count, row_count = feats_ref.shape
    _, source_count, _ = lists_ref.shape
    slabs = row_count // lanes
    feats = feats_ref[0]
    wide = feats.astype(jnp.float32)
    squares = jnp.sum(wide * wide, axis=0, keepdims=True) / (spread * feat_count)
    positions = here() * row_count + lax.broadcasted_iota(jnp.int32, (1, row_count), 1)
    weights = weights_ref[...]
    alive = totals_ref[lax.axis_index("tm")]
    used = (positions < alive) & (weights > 1e-37)
    share = offset - squares + jnp.log(jnp.where(used, weights, 1.0))
    share = lane_blocks(jnp.where(used, share, dead_exponent))
    listed = listed_row(lists_ref[0].astype(jnp.float32))
    shares = pieces(share)
    columns = [feats[:, slab * lanes : (slab + 1) * lanes] for slab in range(slabs)]

    def bundle(first, last):
        rows = [piece[first:last] for piece in shares]
        rows.append(jnp.broadcast_to(listed, (last - first, lanes)))
        tail = jnp.concatenate(rows, axis=0).astype(bf16)
        return jnp.concatenate([*columns[first:last], tail], axis=0)

    whole_ref[...] = bundle(0, slabs)
    facts_ref[...] = stacked_rows([weights, alive.astype(jnp.float32)], 8, row_count)


def rows_kernel(source_count, feat_count, *refs):
    *part_refs, rows_ref = refs
    row_count = rows_ref.shape[0] - list_rows
    slabs = row_count // lanes // len(part_refs)
    feats = [
        part_ref[slab * feat_count : (slab + 1) * feat_count, :]
        for part_ref in part_refs
        for slab in range(slabs)
    ]
    wide = jnp.concatenate(feats, axis=1).astype(jnp.float32)
    squares = jnp.sum(wide * wide, axis=0, keepdims=True) / (spread * feat_count)
    block = lax.broadcasted_iota(jnp.int32, (1, row_count), 1) // (row_count // source_count)
    member = [jnp.where(block == place, 1.0, 0.0) for place in range(source_count)]
    tail = stacked_rows(
        [1.0, 1.0, 1.0, *pieces(-squares), 0.0, 0.0, *member], lanes - feat_count, row_count
    )
    columns = jnp.concatenate([wide * (2.0 / (spread * feat_count)), tail], axis=0)
    rows_ref[:row_count, :] = columns.T.astype(bf16)
    tail = part_refs[0][slabs * feat_count :, :].astype(jnp.float32)
    listed = tail[3 * slabs : 3 * slabs + 1]
    rows_ref[row_count:, :] = jnp.broadcast_to(listed, (list_rows, lanes)).astype(bf16)


def updated(alive, potentials, prior):
    _, row_count = potentials.shape
    positions = here() * row_count + lax.broadcasted_iota(jnp.int32, (1, row_count), 1)
    live = positions.astype(jnp.float32) < alive
    prior = jnp.where(live, prior, 0.0)
    cell_total = row_count * lax.axis_size("cells") * lax.axis_size("feat")
    wanted = cell_total / alive
    scales = potentials * jnp.sqrt(wanted / jnp.where(live, prior, 1.0))
    return jnp.where(live, scales, 0.0), prior


def closed_pairs(sent, own_lists, ours, there, blocks, forward, list_shape):
    source_count, list_len, _ = list_shape
    by_sender = lax.axis_index("tm") > 0 if forward is None else jnp.bool_(forward)
    shape = (len(blocks) * 8, lanes)
    row_ids = lax.broadcasted_iota(jnp.int32, shape, 0)
    other, block = row_ids // 8 + blocks[0], row_ids % 8
    lister = lax.broadcasted_iota(jnp.int32, shape, 1) // list_len
    values = jnp.where(by_sender, sent, own_lists)
    wanted = jnp.where(by_sender, ours * source_count + block, there * source_count + other)
    hit = (values == wanted.astype(jnp.float32)) & (lister == jnp.where(by_sender, other, block))
    found = jnp.max(jnp.where(hit, 1.0, 0.0), axis=1, keepdims=True)
    return jnp.broadcast_to(jnp.where(found > 0.0, 0.0, dead_exponent), shape)


def add_shard(shard_ref, there, part, parts, rows_ref, ours, forward, list_shape, total):
    source_count, _, feat_count = list_shape
    row_count = rows_ref.shape[0] - list_rows
    slabs = row_count // lanes // parts
    blocks = range(source_count // parts * part, source_count // parts * (part + 1))
    tail = shard_ref[slabs * feat_count : slabs * (feat_count + 4), :].astype(jnp.float32)
    own_lists = rows_ref[row_count:, :].astype(jnp.float32)[:1]
    sent = tail[3 * slabs : 3 * slabs + 1]
    closed = closed_pairs(sent, own_lists, ours, there, blocks, forward, list_shape)
    cells = rows_ref[:row_count, : feat_count + 16]
    for start in range(0, slabs, 2):
        other = start * len(blocks) // slabs
        columns = []
        for slab in (start, start + 1):
            share = [tail[piece * slabs + slab : piece * slabs + slab + 1] for piece in range(3)]
            rows = [stacked_rows([*share, 1.0, 1.0, 1.0], 8, lanes), closed[other * 8 : other * 8 + 8]]
            feats = shard_ref[slab * feat_count : (slab + 1) * feat_count, :]
            columns.append(jnp.concatenate([feats, jnp.concatenate(rows, axis=0).astype(bf16)], axis=0))
        exponents = jnp.dot(
            cells, jnp.concatenate(columns, axis=1), preferred_element_type=jnp.float32
        )
        terms = jnp.exp(exponents)
        total = total + terms[:, :lanes] + terms[:, lanes:]
    return total


def sum_kernel(jobs, ours, forward, list_shape, started, finished, *refs):
    shards, (rows_ref, *refs) = refs[: len(jobs)], refs[len(jobs) :]
    total = jnp.zeros((rows_ref.shape[0] - list_rows, lanes), jnp.float32)
    if started:
        total, refs = refs[0][...], refs[1:]
    for shard_ref, (there, part, parts) in zip(shards, jobs):
        total = add_shard(
            shard_ref, there(), part, parts, rows_ref, ours(), forward, list_shape, total
        )
    refs[0][...] = jnp.sum(total.T, axis=0, keepdims=True) if finished else total


def end_kernel(parts, facts_ref, *refs):
    message = refs[0][...]
    for part_ref in refs[1:parts]:
        message = message + part_ref[...]
    scales_ref, prior_ref = refs[parts:]
    potentials = facts_ref[0:1]
    scales_ref[...], prior_ref[...] = updated(facts_ref[1:2], potentials, potentials * message)


def call(kernel, name, out_shapes, operands, spaces=None, scratch=(), exps=0):
    spaces = spaces or [pltpu.VMEM] * len(operands)
    return pl.pallas_call(
        kernel,
        name=name,
        out_shape=out_shapes,
        in_specs=[pl.BlockSpec(memory_space=space) for space in spaces],
        out_specs=jax.tree.map(lambda _: pl.BlockSpec(memory_space=pltpu.VMEM), out_shapes),
        scratch_shapes=scratch,
        compiler_params=pltpu.CompilerParams(vmem_limit_bytes=vmem_bytes),
        cost_estimate=pl.CostEstimate(flops=160 * exps, bytes_accessed=2**17, transcendentals=exps),
    )(*operands)


def exchange(array, route):
    (moves, shift) = route
    times, count, cores = lax.axis_size("tm"), lax.axis_size("cells"), lax.axis_size("feat")
    pairs = [
        ((time * count + place) * cores + core, ((time + move) * count + shift(place)) * cores + core)
        for time in range(times)
        for move in moves
        if 0 <= time + move < times
        for place in range(count)
        for core in range(cores)
    ]
    return lax.ppermute(array, ("tm", "cells", "feat"), pairs)


def swapped(array, swap):
    cores = lax.axis_size("feat")
    return lax.ppermute(array, "feat", [(core, (core + swap) % cores) for core in range(cores)])


def on_device(principal_coordinates, present_potentials, destination_tiles, living_totals):
    _, feat_count, row_count = principal_coordinates.shape
    _, source_count, list_len = destination_tiles.shape
    block_len = row_count // source_count
    offset = 2.0 / spread - math.log(2 * list_len * block_len)
    times = lax.axis_size("tm")
    row = jax.ShapeDtypeStruct((1, row_count), jnp.float32)
    sums = jax.ShapeDtypeStruct((row_count, lanes), jnp.float32)
    payload_rows = (feat_count + 4) * row_count // lanes
    smem, vmem = pltpu.SMEM, pltpu.VMEM

    scratch = [
        smem(living_totals.shape, jnp.int32),
        vmem(principal_coordinates.shape, bf16),
        vmem(present_potentials.shape, jnp.float32),
        vmem(destination_tiles.shape, jnp.int32),
        pltpu.SemaphoreType.DMA((4,)),
    ]

    def in_hbm(*arrays):
        return [pltpu.with_memory_space_constraint(array, pltpu.HBM) for array in arrays]

    def packed(weights):
        return call(
            functools.partial(pack_kernel, offset),
            "pack_cells",
            (
                jax.ShapeDtypeStruct((payload_rows, lanes), bf16),
                jax.ShapeDtypeStruct((8, row_count), jnp.float32),
            ),
            in_hbm(living_totals, principal_coordinates, weights, destination_tiles),
            [pltpu.HBM] * 4,
            scratch,
        )

    count, cores = lax.axis_size("cells"), lax.axis_size("feat")
    xor = count > 1 and count & (count - 1) == 0

    def shifted(distance):
        return lambda place: place ^ distance if xor else (place + distance) % count

    def group_of(distance, swap=0):
        place, core = lax.axis_index("cells"), lax.axis_index("feat")
        source = jnp.bitwise_xor(place, distance) if xor else lax.rem(place + count - distance, count)
        return source * cores + lax.rem(core + cores - swap, cores)

    def cell_rows(parts):
        return call(
            functools.partial(rows_kernel, source_count, feat_count),
            "cell_rows",
            jax.ShapeDtypeStruct((row_count + list_rows, lanes), bf16),
            parts,
        )

    def summed(pack, step):
        payload, _ = pack
        forward = None if step is None else step > 0
        moves = (1, -1) if step is None else (step,)
        *distances, far = range(0, count, 2 if xor else 1)
        far_shard = exchange(payload, (moves, shifted(far)))
        shards = {distance: exchange(payload, (moves, shifted(distance))) for distance in distances}

        def added(jobs, rows, ours, total, finished):
            return call(
                functools.partial(
                    sum_kernel,
                    [place for _, place in jobs],
                    ours,
                    forward,
                    (source_count, list_len, feat_count),
                    total is not None,
                    finished,
                ),
                "sum_tiles",
                row if finished else sums,
                [*(shard for shard, _ in jobs), rows] + ([] if total is None else [total]),
                exps=len(jobs) * row_count * row_count,
            )

        def job(shard, distance, swap, part=0, parts=1):
            here_now = swapped(shard, swap) if swap else shard
            return here_now, (functools.partial(group_of, distance, swap), part, parts)

        def batch(swap):
            return [job(shard, distance, swap) for distance, shard in shards.items()]

        if not xor:
            jobs = [one for swap in range(cores) for one in batch(swap)]
            jobs += [job(far_shard, far, swap) for swap in range(cores)]
            return [added(jobs, cell_rows([payload]), group_of_own, None, True)]

        near = cell_rows([exchange(payload, ((0,), shifted(1)))])
        near_group = functools.partial(group_of, 1)
        own = cell_rows([payload])
        far_job = job(far_shard, far, 0)
        direct = [far_job, *batch(0)]
        crossed = [job(far_shard, far, swap) for swap in range(1, cores)]
        crossed += [one for swap in range(1, cores) for one in batch(swap)]
        total = added(direct, near, near_group, None, False)
        total = added(crossed, near, near_group, total, True)
        own, _ = lax.optimization_barrier((own, total))
        return [
            exchange(total, ((0,), shifted(1))),
            added([*direct, *crossed], own, group_of_own, None, True),
        ]

    group_of_own = functools.partial(group_of, 0)

    if times == 2:
        pack = packed(present_potentials)
        parts = summed(pack, None)
        return tuple(
            call(functools.partial(end_kernel, len(parts)), "end", (row, row), [pack[1], *parts])
        )

    time_here = lax.axis_index("tm")

    def advance(_, state):
        forward, backward = state
        pushed = sum(summed(packed(present_potentials * forward), 1))
        pulled = sum(summed(packed(present_potentials * backward), -1))
        return (
            jnp.where(time_here == 0, 1.0, pushed),
            jnp.where(time_here == times - 1, 1.0, pulled),
        )

    unit = jnp.ones((1, row_count), jnp.float32)
    forward, backward = lax.fori_loop(0, times - 1, advance, (unit, unit))
    return updated(living_totals[time_here].astype(jnp.float32), present_potentials, present_potentials * forward * backward)


def solution(mesh):
    in_specs = (
        P(("runs", "tm"), None, ("cells", "feat")),
        P(("runs", "tm"), ("cells", "feat")),
        P(("runs", "tm"), ("cells", "feat"), None),
        P("runs"),
    )
    out_specs = (P(("runs", "tm"), ("cells", "feat")), P(("runs", "tm"), ("cells", "feat")))
    return jax.shard_map(
        on_device, mesh=mesh, in_specs=in_specs, out_specs=out_specs, check_vma=False
    )
```

```python
import functools
import math

import jax
import jax.numpy as jnp
from jax import lax
from jax.experimental import pallas as pl
from jax.experimental.pallas import tpu as pltpu
from jax.sharding import PartitionSpec as P

spread = 0.5
dead_exponent = -32768.0
vmem_bytes = 32 * 1024 * 1024
lanes = 128
list_rows = 16
bf16 = jnp.bfloat16


def pieces(value):
    high = value.astype(bf16).astype(jnp.float32)
    rest = value - high
    mid = rest.astype(bf16).astype(jnp.float32)
    return high, mid, (rest - mid).astype(bf16).astype(jnp.float32)


def stacked_rows(rows, height, width):
    row_ids = lax.broadcasted_iota(jnp.int32, (height, width), 0)
    block = jnp.zeros((height, width), jnp.float32)
    for place, row in enumerate(rows):
        block = jnp.where(row_ids == place, row, block)
    return block


def lane_blocks(row):
    return jnp.concatenate(
        [row[:, start : start + lanes] for start in range(0, row.shape[1], lanes)], axis=0
    )


def here():
    return lax.axis_index("cells") * lax.axis_size("feat") + lax.axis_index("feat")


def listed_row(lists):
    source_count, list_len = lists.shape
    rows = [lists[place : place + 1] for place in range(source_count)]
    fill = jnp.full((1, lanes - source_count * list_len), -1.0, jnp.float32)
    return jnp.concatenate(rows + [fill], axis=1)


def fetch(sources, targets, sems):
    copies = [
        pltpu.make_async_copy(source, target, sems.at[place])
        for place, (source, target) in enumerate(zip(sources, targets))
    ]
    for copy in copies:
        copy.start()
    for copy in copies:
        copy.wait()


def pack_kernel(
    offset, totals_hbm, feats_hbm, weights_hbm, lists_hbm, payload_ref, facts_ref, *scratch
):
    totals_ref, feats_ref, weights_ref, lists_ref, sems = scratch
    fetch((feats_hbm, weights_hbm, lists_hbm, totals_hbm), (feats_ref, weights_ref, lists_ref, totals_ref), sems)
    _, feat_count, row_count = feats_ref.shape
    _, source_count, _ = lists_ref.shape
    slabs = row_count // lanes
    feats = feats_ref[0]
    wide = feats.astype(jnp.float32)
    squares = lane_blocks(jnp.sum(wide * wide, axis=0, keepdims=True)) / (spread * feat_count)
    shape = (slabs, lanes)
    positions = here() * row_count + lanes * lax.broadcasted_iota(jnp.int32, shape, 0)
    positions = positions + lax.broadcasted_iota(jnp.int32, shape, 1)
    weights = lane_blocks(weights_ref[...])
    alive = totals_ref[lax.axis_index("tm")]
    used = (positions < alive) & (weights > 1e-37)
    share = offset - squares + jnp.log(jnp.where(used, weights, 1.0))
    share = jnp.where(used, share, dead_exponent)
    listed = jnp.broadcast_to(listed_row(lists_ref[0].astype(jnp.float32)), shape)
    tail = jnp.concatenate([*pieces(share), listed], axis=0).astype(bf16)
    columns = [feats[:, slab * lanes : (slab + 1) * lanes] for slab in range(slabs)]
    payload_ref[...] = jnp.concatenate([*columns, tail], axis=0)
    facts_ref[...] = stacked_rows([weights_ref[...], alive.astype(jnp.float32)], 8, row_count)


def rows_kernel(list_shape, payload_ref, rows_ref):
    source_count, _, feat_count = list_shape
    row_count = rows_ref.shape[0] - list_rows
    slabs = row_count // lanes
    feats = [payload_ref[slab * feat_count : (slab + 1) * feat_count, :] for slab in range(slabs)]
    wide = jnp.concatenate(feats, axis=1).astype(jnp.float32)
    squares = jnp.sum(wide * wide, axis=0, keepdims=True) / (spread * feat_count)
    block = lax.broadcasted_iota(jnp.int32, (1, row_count), 1) // (row_count // source_count)
    member = [jnp.where(block == place, 1.0, 0.0) for place in range(source_count)]
    tail = stacked_rows(
        [1.0, 1.0, 1.0, *pieces(-squares), 0.0, 0.0, *member], lanes - feat_count, row_count
    )
    columns = jnp.concatenate([wide * (2.0 / (spread * feat_count)), tail], axis=0)
    rows_ref[:row_count, :] = columns.T.astype(bf16)
    tail = payload_ref[slabs * feat_count :, :].astype(jnp.float32)
    listed = tail[3 * slabs : 3 * slabs + 1]
    rows_ref[row_count:, :] = jnp.broadcast_to(listed, (list_rows, lanes)).astype(bf16)


def updated(alive, potentials, prior):
    _, row_count = potentials.shape
    positions = here() * row_count + lax.broadcasted_iota(jnp.int32, (1, row_count), 1)
    live = positions.astype(jnp.float32) < alive
    prior = jnp.where(live, prior, 0.0)
    cell_total = row_count * lax.axis_size("cells") * lax.axis_size("feat")
    wanted = cell_total / alive
    scales = potentials * jnp.sqrt(wanted / jnp.where(live, prior, 1.0))
    return jnp.where(live, scales, 0.0), prior


def closed_pairs(sent, own_lists, ours, there, forward, list_shape):
    source_count, list_len, _ = list_shape
    by_sender = lax.axis_index("tm") > 0 if forward is None else jnp.bool_(forward)
    shape = (source_count * 8, lanes)
    row_ids = lax.broadcasted_iota(jnp.int32, shape, 0)
    other, block = row_ids // 8, row_ids % 8
    lister = lax.broadcasted_iota(jnp.int32, shape, 1) // list_len
    values = jnp.where(by_sender, sent, own_lists)
    wanted = jnp.where(by_sender, ours * source_count + block, there * source_count + other)
    hit = (values == wanted.astype(jnp.float32)) & (lister == jnp.where(by_sender, other, block))
    found = jnp.max(jnp.where(hit, 1.0, 0.0), axis=1, keepdims=True)
    return jnp.broadcast_to(jnp.where(found > 0.0, 0.0, dead_exponent), shape)


def add_shard(shard_ref, there, rows_ref, ours, forward, list_shape, total):
    source_count, _, feat_count = list_shape
    row_count = rows_ref.shape[0] - list_rows
    slabs = row_count // lanes
    tail = shard_ref[slabs * feat_count :, :].astype(jnp.float32)
    own_lists = rows_ref[row_count:, :].astype(jnp.float32)[:1]
    sent = tail[3 * slabs : 3 * slabs + 1]
    closed = closed_pairs(sent, own_lists, ours, there, forward, list_shape)
    cells = rows_ref[:row_count, : feat_count + 16]
    for start in range(0, slabs, 2):
        other = start * source_count // slabs
        columns = []
        for slab in (start, start + 1):
            share = [tail[piece * slabs + slab : piece * slabs + slab + 1] for piece in range(3)]
            rows = [stacked_rows([*share, 1.0, 1.0, 1.0], 8, lanes), closed[other * 8 : other * 8 + 8]]
            feats = shard_ref[slab * feat_count : (slab + 1) * feat_count, :]
            columns.append(jnp.concatenate([feats, jnp.concatenate(rows, axis=0).astype(bf16)], axis=0))
        exponents = jnp.dot(
            cells, jnp.concatenate(columns, axis=1), preferred_element_type=jnp.float32
        )
        terms = jnp.exp(exponents)
        total = total + terms[:, :lanes] + terms[:, lanes:]
    return total


def sum_kernel(groups, ours, forward, list_shape, built, started, finished, *refs):
    shards, (cells_ref, *refs) = refs[: len(groups)], refs[len(groups) :]
    rows_ref = cells_ref
    if built:
        rows_ref, *refs = refs
        rows_kernel(list_shape, cells_ref, rows_ref)
    total = jnp.zeros((rows_ref.shape[0] - list_rows, lanes), jnp.float32)
    if started:
        total, refs = refs[0][...], refs[1:]
    for shard_ref, there in zip(shards, groups):
        total = add_shard(shard_ref, there(), rows_ref, ours(), forward, list_shape, total)
    refs[0][...] = jnp.sum(total.T, axis=0, keepdims=True) if finished else total


def end_kernel(parts, facts_ref, *refs):
    message = refs[0][...]
    for part_ref in refs[1:parts]:
        message = message + part_ref[...]
    scales_ref, prior_ref = refs[parts:]
    potentials = facts_ref[0:1]
    scales_ref[...], prior_ref[...] = updated(facts_ref[1:2], potentials, potentials * message)


def call(kernel, name, out_shapes, operands, spaces=None, scratch=(), exps=0):
    spaces = spaces or [pltpu.VMEM] * len(operands)
    return pl.pallas_call(
        kernel,
        name=name,
        out_shape=out_shapes,
        in_specs=[pl.BlockSpec(memory_space=space) for space in spaces],
        out_specs=jax.tree.map(lambda _: pl.BlockSpec(memory_space=pltpu.VMEM), out_shapes),
        scratch_shapes=scratch,
        compiler_params=pltpu.CompilerParams(vmem_limit_bytes=vmem_bytes),
        cost_estimate=pl.CostEstimate(flops=160 * exps, bytes_accessed=2**17, transcendentals=exps),
    )(*operands)


def exchange(array, route):
    (moves, shift) = route
    times, count, cores = lax.axis_size("tm"), lax.axis_size("cells"), lax.axis_size("feat")
    pairs = [
        ((time * count + place) * cores + core, ((time + move) * count + shift(place)) * cores + core)
        for time in range(times)
        for move in moves
        if 0 <= time + move < times
        for place in range(count)
        for core in range(cores)
    ]
    return lax.ppermute(array, ("tm", "cells", "feat"), pairs)


def swapped(array, swap):
    cores = lax.axis_size("feat")
    return lax.ppermute(array, "feat", [(core, (core + swap) % cores) for core in range(cores)])


def on_device(principal_coordinates, present_potentials, destination_tiles, living_totals):
    _, feat_count, row_count = principal_coordinates.shape
    _, source_count, list_len = destination_tiles.shape
    block_len = row_count // source_count
    offset = 2.0 / spread - math.log(2 * list_len * block_len)
    times = lax.axis_size("tm")
    row = jax.ShapeDtypeStruct((1, row_count), jnp.float32)
    sums = jax.ShapeDtypeStruct((row_count, lanes), jnp.float32)
    payload_rows = (feat_count + 4) * row_count // lanes
    smem, vmem = pltpu.SMEM, pltpu.VMEM

    scratch = [
        smem(living_totals.shape, jnp.int32),
        vmem(principal_coordinates.shape, bf16),
        vmem(present_potentials.shape, jnp.float32),
        vmem(destination_tiles.shape, jnp.int32),
        pltpu.SemaphoreType.DMA((4,)),
    ]

    def in_hbm(*arrays):
        return [pltpu.with_memory_space_constraint(array, pltpu.HBM) for array in arrays]

    def packed(weights):
        return call(
            functools.partial(pack_kernel, offset),
            "pack_cells",
            (
                jax.ShapeDtypeStruct((payload_rows, lanes), bf16),
                jax.ShapeDtypeStruct((8, row_count), jnp.float32),
            ),
            in_hbm(living_totals, principal_coordinates, weights, destination_tiles),
            [pltpu.HBM] * 4,
            scratch,
        )

    count, cores = lax.axis_size("cells"), lax.axis_size("feat")
    xor = count > 1 and count & (count - 1) == 0

    def shifted(distance):
        return lambda place: place ^ distance if xor else (place + distance) % count

    def group_of(distance, swap=0):
        place, core = lax.axis_index("cells"), lax.axis_index("feat")
        source = jnp.bitwise_xor(place, distance) if xor else lax.rem(place + count - distance, count)
        return source * cores + lax.rem(core + cores - swap, cores)

    list_shape = (source_count, list_len, feat_count)
    rows_shape = jax.ShapeDtypeStruct((row_count + list_rows, lanes), bf16)

    def cell_rows(payload):
        return call(functools.partial(rows_kernel, list_shape), "cell_rows", rows_shape, [payload])

    def summed(pack, step):
        payload, _ = pack
        forward = None if step is None else step > 0
        moves = (1, -1) if step is None else (step,)
        *distances, far = range(0, count, 2 if xor else 1)
        far_shard = exchange(payload, (moves, shifted(far)))
        shards = {distance: exchange(payload, (moves, shifted(distance))) for distance in distances}

        def added(jobs, cells, ours, total=None, finished=False, built=False):
            result = row if finished else sums
            return call(
                functools.partial(
                    sum_kernel,
                    [there for _, there in jobs],
                    ours,
                    forward,
                    list_shape,
                    built,
                    total is not None,
                    finished,
                ),
                "sum_tiles",
                (rows_shape, result) if built else result,
                [*(shard for shard, _ in jobs), cells] + ([] if total is None else [total]),
                exps=len(jobs) * row_count * row_count,
            )

        def job(shard, distance, swap):
            return swapped(shard, swap) if swap else shard, functools.partial(group_of, distance, swap)

        def batch(swap):
            return [job(shard, distance, swap) for distance, shard in shards.items()]

        own = cell_rows(payload)
        if not xor:
            jobs = [one for swap in range(cores) for one in batch(swap)]
            jobs += [job(far_shard, far, swap) for swap in range(cores)]
            return [added(jobs, own, group_of_own, finished=True)]

        near_group = functools.partial(group_of, 1)
        near = exchange(payload, ((0,), shifted(1)))
        ready, _ = lax.optimization_barrier((far_shard, own))
        direct = [job(far_shard, far, 0), *batch(0)]
        crossed = [job(ready, far, swap) for swap in range(1, cores)]
        crossed += [one for swap in range(1, cores) for one in batch(swap)]
        near, total = added(direct, near, near_group, built=True)
        total = added(crossed, near, near_group, total, finished=True)
        own, _ = lax.optimization_barrier((own, total))
        return [
            exchange(total, ((0,), shifted(1))),
            added([*direct, *crossed], own, group_of_own, finished=True),
        ]

    group_of_own = functools.partial(group_of, 0)

    if times == 2:
        pack = packed(present_potentials)
        parts = summed(pack, None)
        return tuple(
            call(functools.partial(end_kernel, len(parts)), "end", (row, row), [pack[1], *parts])
        )

    time_here = lax.axis_index("tm")

    def advance(_, state):
        forward, backward = state
        pushed = sum(summed(packed(present_potentials * forward), 1))
        pulled = sum(summed(packed(present_potentials * backward), -1))
        return (
            jnp.where(time_here == 0, 1.0, pushed),
            jnp.where(time_here == times - 1, 1.0, pulled),
        )

    unit = jnp.ones((1, row_count), jnp.float32)
    forward, backward = lax.fori_loop(0, times - 1, advance, (unit, unit))
    return updated(living_totals[time_here].astype(jnp.float32), present_potentials, present_potentials * forward * backward)


def solution(mesh):
    in_specs = (
        P(("runs", "tm"), None, ("cells", "feat")),
        P(("runs", "tm"), ("cells", "feat")),
        P(("runs", "tm"), ("cells", "feat"), None),
        P("runs"),
    )
    out_specs = (P(("runs", "tm"), ("cells", "feat")), P(("runs", "tm"), ("cells", "feat")))
    return jax.shard_map(
        on_device, mesh=mesh, in_specs=in_specs, out_specs=out_specs, check_vma=False
    )
```

```python
import functools
import math

import jax
import jax.numpy as jnp
from jax import lax
from jax.experimental import pallas as pl
from jax.experimental.pallas import tpu as pltpu
from jax.sharding import PartitionSpec as P

spread = 0.5
dead_exponent = -32768.0
vmem_bytes = 32 * 1024 * 1024
lanes = 128
list_rows = 16
pairs_at_once = 6
feat_copies = 4
bf16 = jnp.bfloat16


def pieces(value):
    high = value.astype(bf16).astype(jnp.float32)
    rest = value - high
    mid = rest.astype(bf16).astype(jnp.float32)
    return high, mid, (rest - mid).astype(bf16).astype(jnp.float32)


def stacked_rows(rows, height, width):
    row_ids = lax.broadcasted_iota(jnp.int32, (height, width), 0)
    block = jnp.zeros((height, width), jnp.float32)
    for place, row in enumerate(rows):
        block = jnp.where(row_ids == place, row, block)
    return block


def lane_blocks(row):
    return jnp.concatenate(
        [row[:, start : start + lanes] for start in range(0, row.shape[1], lanes)], axis=0
    )


def here():
    return lax.axis_index("cells") * lax.axis_size("feat") + lax.axis_index("feat")


def listed_row(lists):
    source_count, list_len = lists.shape
    rows = [lists[place : place + 1] for place in range(source_count)]
    fill = jnp.full((1, lanes - source_count * list_len), -1.0, jnp.float32)
    return jnp.concatenate(rows + [fill], axis=1)


def fetch(sources, targets, sems):
    copies = [
        pltpu.make_async_copy(source, target, sems.at[place])
        for place, (source, target) in enumerate(zip(sources, targets))
    ]
    for copy in copies:
        copy.start()
    for copy in copies:
        copy.wait()


def pack_kernel(
    offset, totals_hbm, feats_hbm, weights_hbm, lists_hbm, payload_ref, facts_ref, *scratch
):
    totals_ref, feats_ref, weights_ref, lists_ref, sems = scratch
    _, feat_count, row_count = feats_ref.shape
    share = feat_count // feat_copies
    parts = [pl.ds(start, share) for start in range(0, feat_count, share)]
    fetch(
        [*(feats_hbm.at[:, part, :] for part in parts), weights_hbm, lists_hbm, totals_hbm],
        [*(feats_ref.at[:, part, :] for part in parts), weights_ref, lists_ref, totals_ref],
        sems,
    )
    _, source_count, _ = lists_ref.shape
    slabs = row_count // lanes
    feats = feats_ref[0]
    wide = feats.astype(jnp.float32)
    squares = lane_blocks(jnp.sum(wide * wide, axis=0, keepdims=True)) / (spread * feat_count)
    shape = (slabs, lanes)
    positions = here() * row_count + lanes * lax.broadcasted_iota(jnp.int32, shape, 0)
    positions = positions + lax.broadcasted_iota(jnp.int32, shape, 1)
    weights = lane_blocks(weights_ref[...])
    alive = totals_ref[lax.axis_index("tm")]
    used = (positions < alive) & (weights > 1e-37)
    share = offset - squares + jnp.log(jnp.where(used, weights, 1.0))
    share = jnp.where(used, share, dead_exponent)
    listed = jnp.broadcast_to(listed_row(lists_ref[0].astype(jnp.float32)), shape)
    tail = jnp.concatenate([*pieces(share), listed], axis=0).astype(bf16)
    columns = [feats[:, slab * lanes : (slab + 1) * lanes] for slab in range(slabs)]
    payload_ref[...] = jnp.concatenate([*columns, tail], axis=0)
    facts_ref[...] = stacked_rows([weights_ref[...], alive.astype(jnp.float32)], 8, row_count)


def rows_kernel(list_shape, payload_ref, rows_ref):
    source_count, _, feat_count = list_shape
    row_count = rows_ref.shape[0] - list_rows
    slabs = row_count // lanes
    feats = [payload_ref[slab * feat_count : (slab + 1) * feat_count, :] for slab in range(slabs)]
    wide = jnp.concatenate(feats, axis=1).astype(jnp.float32)
    squares = jnp.sum(wide * wide, axis=0, keepdims=True) / (spread * feat_count)
    block = lax.broadcasted_iota(jnp.int32, (1, row_count), 1) // (row_count // source_count)
    member = [jnp.where(block == place, 1.0, 0.0) for place in range(source_count)]
    tail = stacked_rows(
        [1.0, 1.0, 1.0, *pieces(-squares), 0.0, 0.0, *member], lanes - feat_count, row_count
    )
    columns = jnp.concatenate([wide * (2.0 / (spread * feat_count)), tail], axis=0)
    rows_ref[:row_count, :] = columns.T.astype(bf16)
    tail = payload_ref[slabs * feat_count :, :].astype(jnp.float32)
    listed = tail[3 * slabs : 3 * slabs + 1]
    rows_ref[row_count:, :] = jnp.broadcast_to(listed, (list_rows, lanes)).astype(bf16)


def updated(alive, potentials, prior):
    _, row_count = potentials.shape
    positions = here() * row_count + lax.broadcasted_iota(jnp.int32, (1, row_count), 1)
    live = positions.astype(jnp.float32) < alive
    prior = jnp.where(live, prior, 0.0)
    cell_total = row_count * lax.axis_size("cells") * lax.axis_size("feat")
    wanted = cell_total / alive
    scales = potentials * jnp.sqrt(wanted / jnp.where(live, prior, 1.0))
    return jnp.where(live, scales, 0.0), prior


def listed_pairs(tails, own_lists, ours, groups, forward, list_shape):
    source_count, list_len, _ = list_shape
    by_sender = lax.axis_index("tm") > 0 if forward is None else jnp.bool_(forward)
    lister = lax.broadcasted_iota(jnp.int32, (1, lanes), 1) // list_len
    found = jnp.zeros((1, lanes), jnp.int32)
    for shard, (sent, there) in enumerate(zip(tails, groups)):
        values = jnp.where(by_sender, sent, own_lists)
        first = jnp.where(by_sender, ours, there) * source_count
        for place in range(source_count):
            bit = jnp.where(by_sender, place * source_count + lister, lister * source_count + place)
            bit = bit + shard * source_count**2
            hit = values == (first + place).astype(jnp.float32)
            found = found + jnp.where(hit, jnp.left_shift(1, bit), 0)
    return jnp.sum(found)


def sum_pairs(shards, groups, rows_ref, ours, forward, list_shape, list_ref, tiles_ref, total_ref):
    source_count, _, feat_count = list_shape
    row_count = rows_ref.shape[0] - list_rows
    block_len = row_count // source_count
    slabs = row_count // lanes
    depth = feat_count + 16
    own_lists = rows_ref[row_count:, :].astype(jnp.float32)[:1]
    tails = []
    for place, shard_ref in enumerate(shards):
        tail = shard_ref[slabs * feat_count :, :].astype(jnp.float32)
        tails.append(tail[3 * slabs : 3 * slabs + 1])
        for slab in range(slabs):
            share = [tail[piece * slabs + slab : piece * slabs + slab + 1] for piece in range(3)]
            rows = stacked_rows([*share, 1.0, 1.0, 1.0], 16, lanes).astype(bf16)
            feats = shard_ref[slab * feat_count : (slab + 1) * feat_count, :]
            start = (place * slabs + slab) * depth
            tiles_ref[start : start + depth, :] = jnp.concatenate([feats, rows], axis=0)
    square = source_count**2
    at_once = 32 // square
    count = jnp.int32(0)
    for first in range(0, len(shards), at_once):
        last = min(first + at_once, len(shards))
        bits = listed_pairs(tails[first:last], own_lists, ours, groups[first:last], forward, list_shape)
        for place in range((last - first) * square):
            list_ref[count] = jnp.int32(first * square + place)
            count = count + jnp.bitwise_and(jnp.right_shift(bits, place), 1)
    pair_total = len(shards) * square
    for place in range(pairs_at_once - 1):
        list_ref[count + place] = jnp.int32(pair_total)

    def step(index, carry):
        sums = []
        for place in range(pairs_at_once):
            listed = list_ref[index * pairs_at_once + place]
            pair = jnp.minimum(listed, pair_total - 1)
            block, other = lax.rem(pair // source_count, source_count), lax.rem(pair, source_count)
            row = pl.multiple_of(block * block_len, block_len)
            tile = (pair // square * source_count + other) * (slabs // source_count) * depth
            columns = [
                tiles_ref[pl.ds(pl.multiple_of(tile + slab * depth, 16), depth), :]
                for slab in range(slabs // source_count)
            ]
            exponents = jnp.dot(
                rows_ref[pl.ds(row, block_len), :depth],
                jnp.concatenate(columns, axis=1),
                preferred_element_type=jnp.float32,
            )
            terms = jnp.exp(exponents)
            added = terms[:, :lanes]
            for start in range(lanes, block_len, lanes):
                added = added + terms[:, start : start + lanes]
            sums.append((jnp.where(listed < pair_total, row, row_count), added))
        for row, added in sums:
            total_ref[pl.ds(pl.multiple_of(row, block_len), block_len), :] += added
        return carry

    lax.fori_loop(0, (count + pairs_at_once - 1) // pairs_at_once, step, 0)


def sum_kernel(groups, ours, forward, list_shape, built, started, finished, *refs):
    *refs, list_ref, tiles_ref, total_ref = refs
    shards, (cells_ref, *refs) = refs[: len(groups)], refs[len(groups) :]
    rows_ref = cells_ref
    if built:
        rows_ref, *refs = refs
        rows_kernel(list_shape, cells_ref, rows_ref)
    row_count = rows_ref.shape[0] - list_rows
    if started:
        total_ref[:row_count, :], refs = refs[0][...], refs[1:]
    else:
        total_ref[:row_count, :] = jnp.zeros((row_count, lanes), jnp.float32)
    theres = [there() for there in groups]
    sum_pairs(shards, theres, rows_ref, ours(), forward, list_shape, list_ref, tiles_ref, total_ref)
    total = total_ref[:row_count, :]
    refs[0][...] = jnp.sum(total.T, axis=0, keepdims=True) if finished else total


def end_kernel(parts, facts_ref, *refs):
    message = refs[0][...]
    for part_ref in refs[1:parts]:
        message = message + part_ref[...]
    scales_ref, prior_ref = refs[parts:]
    potentials = facts_ref[0:1]
    scales_ref[...], prior_ref[...] = updated(facts_ref[1:2], potentials, potentials * message)


def call(kernel, name, out_shapes, operands, spaces=None, scratch=(), exps=0):
    spaces = spaces or [pltpu.VMEM] * len(operands)
    return pl.pallas_call(
        kernel,
        name=name,
        out_shape=out_shapes,
        in_specs=[pl.BlockSpec(memory_space=space) for space in spaces],
        out_specs=jax.tree.map(lambda _: pl.BlockSpec(memory_space=pltpu.VMEM), out_shapes),
        scratch_shapes=scratch,
        compiler_params=pltpu.CompilerParams(vmem_limit_bytes=vmem_bytes),
        cost_estimate=pl.CostEstimate(flops=160 * exps, bytes_accessed=2**17, transcendentals=exps),
    )(*operands)


def exchange(array, route):
    (moves, shift) = route
    times, count, cores = lax.axis_size("tm"), lax.axis_size("cells"), lax.axis_size("feat")
    pairs = [
        ((time * count + place) * cores + core, ((time + move) * count + shift(place)) * cores + core)
        for time in range(times)
        for move in moves
        if 0 <= time + move < times
        for place in range(count)
        for core in range(cores)
    ]
    return lax.ppermute(array, ("tm", "cells", "feat"), pairs)


def swapped(array, swap):
    cores = lax.axis_size("feat")
    return lax.ppermute(array, "feat", [(core, (core + swap) % cores) for core in range(cores)])


def on_device(principal_coordinates, present_potentials, destination_tiles, living_totals):
    _, feat_count, row_count = principal_coordinates.shape
    _, source_count, list_len = destination_tiles.shape
    block_len = row_count // source_count
    offset = 2.0 / spread - math.log(2 * list_len * block_len)
    times = lax.axis_size("tm")
    row = jax.ShapeDtypeStruct((1, row_count), jnp.float32)
    sums = jax.ShapeDtypeStruct((row_count, lanes), jnp.float32)
    payload_rows = (feat_count + 4) * row_count // lanes
    smem, vmem = pltpu.SMEM, pltpu.VMEM

    scratch = [
        smem(living_totals.shape, jnp.int32),
        vmem(principal_coordinates.shape, bf16),
        vmem(present_potentials.shape, jnp.float32),
        vmem(destination_tiles.shape, jnp.int32),
        pltpu.SemaphoreType.DMA((feat_copies + 3,)),
    ]

    def in_hbm(*arrays):
        return [pltpu.with_memory_space_constraint(array, pltpu.HBM) for array in arrays]

    def packed(weights):
        return call(
            functools.partial(pack_kernel, offset),
            "pack_cells",
            (
                jax.ShapeDtypeStruct((payload_rows, lanes), bf16),
                jax.ShapeDtypeStruct((8, row_count), jnp.float32),
            ),
            in_hbm(living_totals, principal_coordinates, weights, destination_tiles),
            [pltpu.HBM] * 4,
            scratch,
        )

    count, cores = lax.axis_size("cells"), lax.axis_size("feat")
    xor = count > 1 and count & (count - 1) == 0

    def shifted(distance):
        return lambda place: place ^ distance if xor else (place + distance) % count

    def group_of(distance, swap=0):
        place, core = lax.axis_index("cells"), lax.axis_index("feat")
        source = jnp.bitwise_xor(place, distance) if xor else lax.rem(place + count - distance, count)
        return source * cores + lax.rem(core + cores - swap, cores)

    list_shape = (source_count, list_len, feat_count)
    rows_shape = jax.ShapeDtypeStruct((row_count + list_rows, lanes), bf16)

    def cell_rows(payload):
        return call(functools.partial(rows_kernel, list_shape), "cell_rows", rows_shape, [payload])

    def summed(pack, step):
        payload, _ = pack
        forward = None if step is None else step > 0
        moves = (1, -1) if step is None else (step,)
        *distances, far = range(0, count, 2 if xor else 1)
        far_shard = exchange(payload, (moves, shifted(far)))
        shards = {distance: exchange(payload, (moves, shifted(distance))) for distance in distances}

        def added(jobs, cells, ours, total=None, finished=False, built=False):
            result = row if finished else sums
            return call(
                functools.partial(
                    sum_kernel,
                    [there for _, there in jobs],
                    ours,
                    forward,
                    list_shape,
                    built,
                    total is not None,
                    finished,
                ),
                "sum_tiles",
                (rows_shape, result) if built else result,
                [*(shard for shard, _ in jobs), cells] + ([] if total is None else [total]),
                scratch=[
                    smem((len(jobs) * source_count**2 + pairs_at_once,), jnp.int32),
                    vmem((len(jobs) * (feat_count + 16) * row_count // lanes, lanes), bf16),
                    vmem((row_count + block_len, lanes), jnp.float32),
                ],
                exps=len(jobs) * row_count * row_count,
            )

        def job(shard, distance, swap):
            return swapped(shard, swap) if swap else shard, functools.partial(group_of, distance, swap)

        def batch(swap):
            return [job(shard, distance, swap) for distance, shard in shards.items()]

        own = cell_rows(payload)
        if not xor:
            jobs = [one for swap in range(cores) for one in batch(swap)]
            jobs += [job(far_shard, far, swap) for swap in range(cores)]
            return [added(jobs, own, group_of_own, finished=True)]

        near_group = functools.partial(group_of, 1)
        near = exchange(payload, ((0,), shifted(1)))
        ready, _ = lax.optimization_barrier((far_shard, own))
        direct = [job(far_shard, far, 0), *batch(0)]
        crossed = [job(ready, far, swap) for swap in range(1, cores)]
        crossed += [one for swap in range(1, cores) for one in batch(swap)]
        near, total = added(direct, near, near_group, built=True)
        total = added(crossed, near, near_group, total, finished=True)
        own, _ = lax.optimization_barrier((own, total))
        return [
            exchange(total, ((0,), shifted(1))),
            added([*direct, *crossed], own, group_of_own, finished=True),
        ]

    group_of_own = functools.partial(group_of, 0)

    if times == 2:
        pack = packed(present_potentials)
        parts = summed(pack, None)
        return tuple(
            call(functools.partial(end_kernel, len(parts)), "end", (row, row), [pack[1], *parts])
        )

    time_here = lax.axis_index("tm")

    def advance(_, state):
        forward, backward = state
        pushed = sum(summed(packed(present_potentials * forward), 1))
        pulled = sum(summed(packed(present_potentials * backward), -1))
        return (
            jnp.where(time_here == 0, 1.0, pushed),
            jnp.where(time_here == times - 1, 1.0, pulled),
        )

    unit = jnp.ones((1, row_count), jnp.float32)
    forward, backward = lax.fori_loop(0, times - 1, advance, (unit, unit))
    return updated(living_totals[time_here].astype(jnp.float32), present_potentials, present_potentials * forward * backward)


def solution(mesh):
    in_specs = (
        P(("runs", "tm"), None, ("cells", "feat")),
        P(("runs", "tm"), ("cells", "feat")),
        P(("runs", "tm"), ("cells", "feat"), None),
        P("runs"),
    )
    out_specs = (P(("runs", "tm"), ("cells", "feat")), P(("runs", "tm"), ("cells", "feat")))
    return jax.shard_map(
        on_device, mesh=mesh, in_specs=in_specs, out_specs=out_specs, check_vma=False
    )
```

```python
import functools
import math

import jax
import jax.numpy as jnp
from jax import lax
from jax.experimental import pallas as pl
from jax.experimental.pallas import tpu as pltpu
from jax.sharding import PartitionSpec as P

spread = 0.5
dead_exponent = -32768.0
vmem_bytes = 32 * 1024 * 1024
lanes = 128
list_rows = 16
pairs_at_once = 6
feat_copies = 4
bf16 = jnp.bfloat16


def pieces(value):
    high = value.astype(bf16).astype(jnp.float32)
    rest = value - high
    mid = rest.astype(bf16).astype(jnp.float32)
    return high, mid, (rest - mid).astype(bf16).astype(jnp.float32)


def stacked_rows(rows, height, width):
    row_ids = lax.broadcasted_iota(jnp.int32, (height, width), 0)
    block = jnp.zeros((height, width), jnp.float32)
    for place, row in enumerate(rows):
        block = jnp.where(row_ids == place, row, block)
    return block


def lane_blocks(row):
    return jnp.concatenate(
        [row[:, start : start + lanes] for start in range(0, row.shape[1], lanes)], axis=0
    )


def here():
    return lax.axis_index("cells") * lax.axis_size("feat") + lax.axis_index("feat")


def listed_row(lists):
    source_count, list_len = lists.shape
    rows = [lists[place : place + 1] for place in range(source_count)]
    fill = jnp.full((1, lanes - source_count * list_len), -1.0, jnp.float32)
    return jnp.concatenate(rows + [fill], axis=1)


def fetch(sources, targets, sems):
    copies = [
        pltpu.make_async_copy(source, target, sems.at[place])
        for place, (source, target) in enumerate(zip(sources, targets))
    ]
    for copy in copies:
        copy.start()
    for copy in copies:
        copy.wait()


def pack_kernel(
    offset, totals_hbm, feats_hbm, weights_hbm, lists_hbm, payload_ref, facts_ref, *scratch
):
    totals_ref, feats_ref, weights_ref, lists_ref, sems = scratch
    _, feat_count, row_count = feats_ref.shape
    share = feat_count // feat_copies
    parts = [pl.ds(start, share) for start in range(0, feat_count, share)]
    fetch(
        [*(feats_hbm.at[:, part, :] for part in parts), weights_hbm, lists_hbm, totals_hbm],
        [*(feats_ref.at[:, part, :] for part in parts), weights_ref, lists_ref, totals_ref],
        sems,
    )
    _, source_count, _ = lists_ref.shape
    slabs = row_count // lanes
    feats = feats_ref[0]
    wide = feats.astype(jnp.float32)
    squares = lane_blocks(jnp.sum(wide * wide, axis=0, keepdims=True)) / (spread * feat_count)
    shape = (slabs, lanes)
    positions = here() * row_count + lanes * lax.broadcasted_iota(jnp.int32, shape, 0)
    positions = positions + lax.broadcasted_iota(jnp.int32, shape, 1)
    weights = lane_blocks(weights_ref[...])
    alive = totals_ref[lax.axis_index("tm")]
    used = (positions < alive) & (weights > 1e-37)
    share = offset - squares + jnp.log(jnp.where(used, weights, 1.0))
    share = jnp.where(used, share, dead_exponent)
    listed = jnp.broadcast_to(listed_row(lists_ref[0].astype(jnp.float32)), shape)
    tail = jnp.concatenate([*pieces(share), listed], axis=0).astype(bf16)
    columns = [feats[:, slab * lanes : (slab + 1) * lanes] for slab in range(slabs)]
    payload_ref[...] = jnp.concatenate([*columns, tail], axis=0)
    facts_ref[...] = stacked_rows([weights_ref[...], alive.astype(jnp.float32)], 8, row_count)


def rows_kernel(list_shape, payload_ref, rows_ref):
    source_count, _, feat_count = list_shape
    row_count = rows_ref.shape[0] - list_rows
    slabs = row_count // lanes
    feats = [payload_ref[slab * feat_count : (slab + 1) * feat_count, :] for slab in range(slabs)]
    wide = jnp.concatenate(feats, axis=1).astype(jnp.float32)
    squares = jnp.sum(wide * wide, axis=0, keepdims=True) / (spread * feat_count)
    block = lax.broadcasted_iota(jnp.int32, (1, row_count), 1) // (row_count // source_count)
    member = [jnp.where(block == place, 1.0, 0.0) for place in range(source_count)]
    tail = stacked_rows(
        [1.0, 1.0, 1.0, *pieces(-squares), 0.0, 0.0, *member], lanes - feat_count, row_count
    )
    columns = jnp.concatenate([wide * (2.0 / (spread * feat_count)), tail], axis=0)
    rows_ref[:row_count, :] = columns.T.astype(bf16)
    tail = payload_ref[slabs * feat_count :, :].astype(jnp.float32)
    listed = tail[3 * slabs : 3 * slabs + 1]
    rows_ref[row_count:, :] = jnp.broadcast_to(listed, (list_rows, lanes)).astype(bf16)


def updated(alive, potentials, prior):
    _, row_count = potentials.shape
    positions = here() * row_count + lax.broadcasted_iota(jnp.int32, (1, row_count), 1)
    live = positions.astype(jnp.float32) < alive
    prior = jnp.where(live, prior, 0.0)
    cell_total = row_count * lax.axis_size("cells") * lax.axis_size("feat")
    wanted = cell_total / alive
    scales = potentials * jnp.sqrt(wanted / jnp.where(live, prior, 1.0))
    return jnp.where(live, scales, 0.0), prior


def listed_pairs(tails, own_lists, ours, groups, forward, list_shape):
    source_count, list_len, _ = list_shape
    by_sender = lax.axis_index("tm") > 0 if forward is None else jnp.bool_(forward)
    lister = lax.broadcasted_iota(jnp.int32, (1, lanes), 1) // list_len
    found = jnp.zeros((1, lanes), jnp.int32)
    for shard, (sent, there) in enumerate(zip(tails, groups)):
        values = jnp.where(by_sender, sent, own_lists)
        first = jnp.where(by_sender, ours, there) * source_count
        for place in range(source_count):
            bit = jnp.where(by_sender, place * source_count + lister, lister * source_count + place)
            bit = bit + shard * source_count**2
            hit = values == (first + place).astype(jnp.float32)
            found = found + jnp.where(hit, jnp.left_shift(1, bit), 0)
    return jnp.sum(found)


def sum_pairs(shards, groups, rows_ref, ours, forward, list_shape, list_ref, tiles_ref, total_ref):
    source_count, _, feat_count = list_shape
    row_count = rows_ref.shape[0] - list_rows
    block_len = row_count // source_count
    slabs = row_count // lanes
    depth = feat_count + 16
    own_lists = rows_ref[row_count:, :].astype(jnp.float32)[:1]
    tails = []
    for place, shard_ref in enumerate(shards):
        tail = shard_ref[slabs * feat_count :, :].astype(jnp.float32)
        tails.append(tail[3 * slabs : 3 * slabs + 1])
        for slab in range(slabs):
            share = [tail[piece * slabs + slab : piece * slabs + slab + 1] for piece in range(3)]
            rows = stacked_rows([*share, 1.0, 1.0, 1.0], 16, lanes).astype(bf16)
            feats = shard_ref[slab * feat_count : (slab + 1) * feat_count, :]
            start = (place * slabs + slab) * depth
            tiles_ref[start : start + depth, :] = jnp.concatenate([feats, rows], axis=0)
    square = source_count**2
    at_once = 32 // square
    count = jnp.int32(0)
    for first in range(0, len(shards), at_once):
        last = min(first + at_once, len(shards))
        bits = listed_pairs(tails[first:last], own_lists, ours, groups[first:last], forward, list_shape)
        for place in range((last - first) * square):
            list_ref[count] = jnp.int32(first * square + place)
            count = count + jnp.bitwise_and(jnp.right_shift(bits, place), 1)
    pair_total = len(shards) * square
    for place in range(pairs_at_once - 1):
        list_ref[count + place] = jnp.int32(pair_total)

    def step(taken, size):
        sums = []
        for place in range(size):
            listed = list_ref[taken + place]
            pair = jnp.minimum(listed, pair_total - 1)
            block, other = lax.rem(pair // source_count, source_count), lax.rem(pair, source_count)
            row = pl.multiple_of(block * block_len, block_len)
            tile = (pair // square * source_count + other) * (slabs // source_count) * depth
            columns = [
                tiles_ref[pl.ds(pl.multiple_of(tile + slab * depth, 16), depth), :]
                for slab in range(slabs // source_count)
            ]
            exponents = jnp.dot(
                rows_ref[pl.ds(row, block_len), :depth],
                jnp.concatenate(columns, axis=1),
                preferred_element_type=jnp.float32,
            )
            terms = jnp.exp(exponents)
            added = terms[:, :lanes]
            for start in range(lanes, block_len, lanes):
                added = added + terms[:, start : start + lanes]
            sums.append((jnp.where(listed < pair_total, row, row_count), added))
        for row, added in sums:
            total_ref[pl.ds(pl.multiple_of(row, block_len), block_len), :] += added

    def whole_step(index, carry):
        step(index * pairs_at_once, pairs_at_once)
        return carry

    half = pairs_at_once // 2
    whole_steps = (count + pairs_at_once - 1 - half) // pairs_at_once
    lax.fori_loop(0, whole_steps, whole_step, 0)

    @pl.when(count > whole_steps * pairs_at_once)
    def _():
        step(whole_steps * pairs_at_once, half)


def sum_kernel(groups, ours, forward, list_shape, built, started, finished, *refs):
    *refs, list_ref, tiles_ref, total_ref = refs
    shards, (cells_ref, *refs) = refs[: len(groups)], refs[len(groups) :]
    rows_ref = cells_ref
    if built:
        rows_ref, *refs = refs
        rows_kernel(list_shape, cells_ref, rows_ref)
    row_count = rows_ref.shape[0] - list_rows
    if started:
        total_ref[:row_count, :], refs = refs[0][...], refs[1:]
    else:
        total_ref[:row_count, :] = jnp.zeros((row_count, lanes), jnp.float32)
    theres = [there() for there in groups]
    sum_pairs(shards, theres, rows_ref, ours(), forward, list_shape, list_ref, tiles_ref, total_ref)
    total = total_ref[:row_count, :]
    refs[0][...] = jnp.sum(total.T, axis=0, keepdims=True) if finished else total


def end_kernel(parts, facts_ref, *refs):
    message = refs[0][...]
    for part_ref in refs[1:parts]:
        message = message + part_ref[...]
    scales_ref, prior_ref = refs[parts:]
    potentials = facts_ref[0:1]
    scales_ref[...], prior_ref[...] = updated(facts_ref[1:2], potentials, potentials * message)


def call(kernel, name, out_shapes, operands, spaces=None, scratch=(), exps=0):
    spaces = spaces or [pltpu.VMEM] * len(operands)
    return pl.pallas_call(
        kernel,
        name=name,
        out_shape=out_shapes,
        in_specs=[pl.BlockSpec(memory_space=space) for space in spaces],
        out_specs=jax.tree.map(lambda _: pl.BlockSpec(memory_space=pltpu.VMEM), out_shapes),
        scratch_shapes=scratch,
        compiler_params=pltpu.CompilerParams(vmem_limit_bytes=vmem_bytes),
        cost_estimate=pl.CostEstimate(flops=160 * exps, bytes_accessed=2**17, transcendentals=exps),
    )(*operands)


def exchange(array, route):
    (moves, shift) = route
    times, count, cores = lax.axis_size("tm"), lax.axis_size("cells"), lax.axis_size("feat")
    pairs = [
        ((time * count + place) * cores + core, ((time + move) * count + shift(place)) * cores + core)
        for time in range(times)
        for move in moves
        if 0 <= time + move < times
        for place in range(count)
        for core in range(cores)
    ]
    return lax.ppermute(array, ("tm", "cells", "feat"), pairs)


def swapped(array, swap):
    cores = lax.axis_size("feat")
    return lax.ppermute(array, "feat", [(core, (core + swap) % cores) for core in range(cores)])


def on_device(principal_coordinates, present_potentials, destination_tiles, living_totals):
    _, feat_count, row_count = principal_coordinates.shape
    _, source_count, list_len = destination_tiles.shape
    block_len = row_count // source_count
    offset = 2.0 / spread - math.log(2 * list_len * block_len)
    times = lax.axis_size("tm")
    row = jax.ShapeDtypeStruct((1, row_count), jnp.float32)
    sums = jax.ShapeDtypeStruct((row_count, lanes), jnp.float32)
    payload_rows = (feat_count + 4) * row_count // lanes
    smem, vmem = pltpu.SMEM, pltpu.VMEM

    scratch = [
        smem(living_totals.shape, jnp.int32),
        vmem(principal_coordinates.shape, bf16),
        vmem(present_potentials.shape, jnp.float32),
        vmem(destination_tiles.shape, jnp.int32),
        pltpu.SemaphoreType.DMA((feat_copies + 3,)),
    ]

    def in_hbm(*arrays):
        return [pltpu.with_memory_space_constraint(array, pltpu.HBM) for array in arrays]

    def packed(weights):
        return call(
            functools.partial(pack_kernel, offset),
            "pack_cells",
            (
                jax.ShapeDtypeStruct((payload_rows, lanes), bf16),
                jax.ShapeDtypeStruct((8, row_count), jnp.float32),
            ),
            in_hbm(living_totals, principal_coordinates, weights, destination_tiles),
            [pltpu.HBM] * 4,
            scratch,
        )

    count, cores = lax.axis_size("cells"), lax.axis_size("feat")
    xor = count > 1 and count & (count - 1) == 0

    def shifted(distance):
        return lambda place: place ^ distance if xor else (place + distance) % count

    def group_of(distance, swap=0):
        place, core = lax.axis_index("cells"), lax.axis_index("feat")
        source = jnp.bitwise_xor(place, distance) if xor else lax.rem(place + count - distance, count)
        return source * cores + lax.rem(core + cores - swap, cores)

    list_shape = (source_count, list_len, feat_count)
    rows_shape = jax.ShapeDtypeStruct((row_count + list_rows, lanes), bf16)

    def cell_rows(payload):
        return call(functools.partial(rows_kernel, list_shape), "cell_rows", rows_shape, [payload])

    def summed(pack, step):
        payload, _ = pack
        forward = None if step is None else step > 0
        moves = (1, -1) if step is None else (step,)
        *distances, far = range(0, count, 2 if xor else 1)
        far_shard = exchange(payload, (moves, shifted(far)))
        shards = {distance: exchange(payload, (moves, shifted(distance))) for distance in distances}

        def added(jobs, cells, ours, total=None, finished=False, built=False):
            result = row if finished else sums
            return call(
                functools.partial(
                    sum_kernel,
                    [there for _, there in jobs],
                    ours,
                    forward,
                    list_shape,
                    built,
                    total is not None,
                    finished,
                ),
                "sum_tiles",
                (rows_shape, result) if built else result,
                [*(shard for shard, _ in jobs), cells] + ([] if total is None else [total]),
                scratch=[
                    smem((len(jobs) * source_count**2 + pairs_at_once,), jnp.int32),
                    vmem((len(jobs) * (feat_count + 16) * row_count // lanes, lanes), bf16),
                    vmem((row_count + block_len, lanes), jnp.float32),
                ],
                exps=len(jobs) * row_count * row_count,
            )

        def job(shard, distance, swap):
            return swapped(shard, swap) if swap else shard, functools.partial(group_of, distance, swap)

        def batch(swap):
            return [job(shard, distance, swap) for distance, shard in shards.items()]

        own = cell_rows(payload)
        if not xor:
            jobs = [one for swap in range(cores) for one in batch(swap)]
            jobs += [job(far_shard, far, swap) for swap in range(cores)]
            return [added(jobs, own, group_of_own, finished=True)]

        near_group = functools.partial(group_of, 1)
        near = exchange(payload, ((0,), shifted(1)))
        ready, _ = lax.optimization_barrier((far_shard, own))
        direct = [job(far_shard, far, 0), *batch(0)]
        crossed = [job(ready, far, swap) for swap in range(1, cores)]
        crossed += [one for swap in range(1, cores) for one in batch(swap)]
        near, total = added(direct, near, near_group, built=True)
        total = added(crossed, near, near_group, total, finished=True)
        own, _ = lax.optimization_barrier((own, total))
        return [
            exchange(total, ((0,), shifted(1))),
            added([*direct, *crossed], own, group_of_own, finished=True),
        ]

    group_of_own = functools.partial(group_of, 0)

    if times == 2:
        pack = packed(present_potentials)
        parts = summed(pack, None)
        return tuple(
            call(functools.partial(end_kernel, len(parts)), "end", (row, row), [pack[1], *parts])
        )

    time_here = lax.axis_index("tm")

    def advance(_, state):
        forward, backward = state
        pushed = sum(summed(packed(present_potentials * forward), 1))
        pulled = sum(summed(packed(present_potentials * backward), -1))
        return (
            jnp.where(time_here == 0, 1.0, pushed),
            jnp.where(time_here == times - 1, 1.0, pulled),
        )

    unit = jnp.ones((1, row_count), jnp.float32)
    forward, backward = lax.fori_loop(0, times - 1, advance, (unit, unit))
    return updated(living_totals[time_here].astype(jnp.float32), present_potentials, present_potentials * forward * backward)


def solution(mesh):
    in_specs = (
        P(("runs", "tm"), None, ("cells", "feat")),
        P(("runs", "tm"), ("cells", "feat")),
        P(("runs", "tm"), ("cells", "feat"), None),
        P("runs"),
    )
    out_specs = (P(("runs", "tm"), ("cells", "feat")), P(("runs", "tm"), ("cells", "feat")))
    return jax.shard_map(
        on_device, mesh=mesh, in_specs=in_specs, out_specs=out_specs, check_vma=False
    )
```

```python
import functools
import math

import jax
import jax.numpy as jnp
from jax import lax
from jax.experimental import pallas as pl
from jax.experimental.pallas import tpu as pltpu
from jax.sharding import PartitionSpec as P

spread = 0.5
dead_exponent = -32768.0
vmem_bytes = 32 * 1024 * 1024
lanes = 128
list_rows = 16
pairs_at_once = 6
feat_copies = 4
bf16 = jnp.bfloat16


def pieces(value):
    high = value.astype(bf16).astype(jnp.float32)
    rest = value - high
    mid = rest.astype(bf16).astype(jnp.float32)
    return high, mid, (rest - mid).astype(bf16).astype(jnp.float32)


def stacked_rows(rows, height, width):
    row_ids = lax.broadcasted_iota(jnp.int32, (height, width), 0)
    block = jnp.zeros((height, width), jnp.float32)
    for place, row in enumerate(rows):
        block = jnp.where(row_ids == place, row, block)
    return block


def lane_blocks(row):
    return jnp.concatenate(
        [row[:, start : start + lanes] for start in range(0, row.shape[1], lanes)], axis=0
    )


def here():
    return lax.axis_index("cells") * lax.axis_size("feat") + lax.axis_index("feat")


def listed_row(lists):
    source_count, list_len = lists.shape
    rows = [lists[place : place + 1] for place in range(source_count)]
    fill = jnp.full((1, lanes - source_count * list_len), -1.0, jnp.float32)
    return jnp.concatenate(rows + [fill], axis=1)


def fetch(sources, targets, sems):
    copies = [
        pltpu.make_async_copy(source, target, sems.at[place])
        for place, (source, target) in enumerate(zip(sources, targets))
    ]
    for copy in copies:
        copy.start()
    for copy in copies:
        copy.wait()


def pack_kernel(
    offset, totals_hbm, feats_hbm, weights_hbm, lists_hbm, payload_ref, near_ref, facts_ref, *scratch
):
    totals_ref, feats_ref, weights_ref, lists_ref, sems = scratch
    _, feat_count, row_count = feats_ref.shape
    share = feat_count // feat_copies
    parts = [pl.ds(start, share) for start in range(0, feat_count, share)]
    fetch(
        [*(feats_hbm.at[:, part, :] for part in parts), weights_hbm, lists_hbm, totals_hbm],
        [*(feats_ref.at[:, part, :] for part in parts), weights_ref, lists_ref, totals_ref],
        sems,
    )
    _, source_count, _ = lists_ref.shape
    slabs = row_count // lanes
    feats = feats_ref[0]
    wide = feats.astype(jnp.float32)
    squares = lane_blocks(jnp.sum(wide * wide, axis=0, keepdims=True)) / (spread * feat_count)
    shape = (slabs, lanes)
    positions = here() * row_count + lanes * lax.broadcasted_iota(jnp.int32, shape, 0)
    positions = positions + lax.broadcasted_iota(jnp.int32, shape, 1)
    weights = lane_blocks(weights_ref[...])
    alive = totals_ref[lax.axis_index("tm")]
    used = (positions < alive) & (weights > 1e-37)
    share = offset - squares + jnp.log(jnp.where(used, weights, 1.0))
    share = jnp.where(used, share, dead_exponent)
    listed = jnp.broadcast_to(listed_row(lists_ref[0].astype(jnp.float32)), shape)
    tail = jnp.concatenate([*pieces(share), listed], axis=0).astype(bf16)
    columns = [feats[:, slab * lanes : (slab + 1) * lanes] for slab in range(slabs)]
    payload_ref[...] = jnp.concatenate([*columns, tail], axis=0)
    near_tail = jnp.broadcast_to(listed[:1], (list_rows, lanes)).astype(bf16)
    near_ref[...] = jnp.concatenate([*columns, near_tail], axis=0)
    facts_ref[...] = stacked_rows([weights_ref[...], alive.astype(jnp.float32)], 8, row_count)


def rows_kernel(list_shape, payload_ref, rows_ref):
    source_count, _, feat_count = list_shape
    row_count = rows_ref.shape[0] - list_rows
    slabs = row_count // lanes
    feats = [payload_ref[slab * feat_count : (slab + 1) * feat_count, :] for slab in range(slabs)]
    wide = jnp.concatenate(feats, axis=1).astype(jnp.float32)
    squares = jnp.sum(wide * wide, axis=0, keepdims=True) / (spread * feat_count)
    block = lax.broadcasted_iota(jnp.int32, (1, row_count), 1) // (row_count // source_count)
    member = [jnp.where(block == place, 1.0, 0.0) for place in range(source_count)]
    tail = stacked_rows(
        [1.0, 1.0, 1.0, *pieces(-squares), 0.0, 0.0, *member], lanes - feat_count, row_count
    )
    columns = jnp.concatenate([wide * (2.0 / (spread * feat_count)), tail], axis=0)
    rows_ref[:row_count, :] = columns.T.astype(bf16)
    height = payload_ref.shape[0]
    listed = payload_ref[height - list_rows :, :].astype(jnp.float32)[list_rows - 1 :]
    rows_ref[row_count:, :] = jnp.broadcast_to(listed, (list_rows, lanes)).astype(bf16)


def updated(alive, potentials, prior):
    _, row_count = potentials.shape
    positions = here() * row_count + lax.broadcasted_iota(jnp.int32, (1, row_count), 1)
    live = positions.astype(jnp.float32) < alive
    prior = jnp.where(live, prior, 0.0)
    cell_total = row_count * lax.axis_size("cells") * lax.axis_size("feat")
    wanted = cell_total / alive
    scales = potentials * jnp.sqrt(wanted / jnp.where(live, prior, 1.0))
    return jnp.where(live, scales, 0.0), prior


def listed_pairs(tails, own_lists, ours, groups, forward, list_shape):
    source_count, list_len, _ = list_shape
    by_sender = lax.axis_index("tm") > 0 if forward is None else jnp.bool_(forward)
    lister = lax.broadcasted_iota(jnp.int32, (1, lanes), 1) // list_len
    found = jnp.zeros((1, lanes), jnp.int32)
    for shard, (sent, there) in enumerate(zip(tails, groups)):
        values = jnp.where(by_sender, sent, own_lists)
        first = jnp.where(by_sender, ours, there) * source_count
        for place in range(source_count):
            bit = jnp.where(by_sender, place * source_count + lister, lister * source_count + place)
            bit = bit + shard * source_count**2
            hit = values == (first + place).astype(jnp.float32)
            found = found + jnp.where(hit, jnp.left_shift(1, bit), 0)
    return jnp.sum(found)


def sum_pairs(shards, groups, rows_ref, ours, forward, list_shape, list_ref, tiles_ref, total_ref):
    source_count, _, feat_count = list_shape
    row_count = rows_ref.shape[0] - list_rows
    block_len = row_count // source_count
    slabs = row_count // lanes
    depth = feat_count + 16
    own_lists = rows_ref[row_count:, :].astype(jnp.float32)[:1]
    tails = []
    for place, shard_ref in enumerate(shards):
        tail = shard_ref[slabs * feat_count :, :].astype(jnp.float32)
        tails.append(tail[3 * slabs : 3 * slabs + 1])
        for slab in range(slabs):
            share = [tail[piece * slabs + slab : piece * slabs + slab + 1] for piece in range(3)]
            rows = stacked_rows([*share, 1.0, 1.0, 1.0], 16, lanes).astype(bf16)
            feats = shard_ref[slab * feat_count : (slab + 1) * feat_count, :]
            start = (place * slabs + slab) * depth
            tiles_ref[start : start + depth, :] = jnp.concatenate([feats, rows], axis=0)
    square = source_count**2
    at_once = 32 // square
    count = jnp.int32(0)
    for first in range(0, len(shards), at_once):
        last = min(first + at_once, len(shards))
        bits = listed_pairs(tails[first:last], own_lists, ours, groups[first:last], forward, list_shape)
        for place in range((last - first) * square):
            list_ref[count] = jnp.int32(first * square + place)
            count = count + jnp.bitwise_and(jnp.right_shift(bits, place), 1)
    pair_total = len(shards) * square
    for place in range(pairs_at_once - 1):
        list_ref[count + place] = jnp.int32(pair_total)

    def step(index, carry):
        sums = []
        for place in range(pairs_at_once):
            listed = list_ref[index * pairs_at_once + place]
            pair = jnp.minimum(listed, pair_total - 1)
            block, other = lax.rem(pair // source_count, source_count), lax.rem(pair, source_count)
            row = pl.multiple_of(block * block_len, block_len)
            tile = (pair // square * source_count + other) * (slabs // source_count) * depth
            columns = [
                tiles_ref[pl.ds(pl.multiple_of(tile + slab * depth, 16), depth), :]
                for slab in range(slabs // source_count)
            ]
            exponents = jnp.dot(
                rows_ref[pl.ds(row, block_len), :depth],
                jnp.concatenate(columns, axis=1),
                preferred_element_type=jnp.float32,
            )
            terms = jnp.exp(exponents)
            added = terms[:, :lanes]
            for start in range(lanes, block_len, lanes):
                added = added + terms[:, start : start + lanes]
            sums.append((jnp.where(listed < pair_total, row, row_count), added))
        for row, added in sums:
            total_ref[pl.ds(pl.multiple_of(row, block_len), block_len), :] += added
        return carry

    lax.fori_loop(0, (count + pairs_at_once - 1) // pairs_at_once, step, 0)


def sum_kernel(groups, ours, forward, list_shape, built, started, finished, *refs):
    *refs, list_ref, tiles_ref, total_ref = refs
    shards, (cells_ref, *refs) = refs[: len(groups)], refs[len(groups) :]
    rows_ref = cells_ref
    if built:
        rows_ref, *refs = refs
        rows_kernel(list_shape, cells_ref, rows_ref)
    row_count = rows_ref.shape[0] - list_rows
    if started:
        total_ref[:row_count, :], refs = refs[0][...], refs[1:]
    else:
        total_ref[:row_count, :] = jnp.zeros((row_count, lanes), jnp.float32)
    theres = [there() for there in groups]
    sum_pairs(shards, theres, rows_ref, ours(), forward, list_shape, list_ref, tiles_ref, total_ref)
    total = total_ref[:row_count, :]
    refs[0][...] = jnp.sum(total.T, axis=0, keepdims=True) if finished else total


def end_kernel(parts, facts_ref, *refs):
    message = refs[0][...]
    for part_ref in refs[1:parts]:
        message = message + part_ref[...]
    scales_ref, prior_ref = refs[parts:]
    potentials = facts_ref[0:1]
    scales_ref[...], prior_ref[...] = updated(facts_ref[1:2], potentials, potentials * message)


def call(kernel, name, out_shapes, operands, spaces=None, scratch=(), exps=0):
    spaces = spaces or [pltpu.VMEM] * len(operands)
    return pl.pallas_call(
        kernel,
        name=name,
        out_shape=out_shapes,
        in_specs=[pl.BlockSpec(memory_space=space) for space in spaces],
        out_specs=jax.tree.map(lambda _: pl.BlockSpec(memory_space=pltpu.VMEM), out_shapes),
        scratch_shapes=scratch,
        compiler_params=pltpu.CompilerParams(vmem_limit_bytes=vmem_bytes),
        cost_estimate=pl.CostEstimate(flops=160 * exps, bytes_accessed=2**17, transcendentals=exps),
    )(*operands)


def exchange(array, route):
    (moves, shift) = route
    times, count, cores = lax.axis_size("tm"), lax.axis_size("cells"), lax.axis_size("feat")
    pairs = [
        ((time * count + place) * cores + core, ((time + move) * count + shift(place)) * cores + core)
        for time in range(times)
        for move in moves
        if 0 <= time + move < times
        for place in range(count)
        for core in range(cores)
    ]
    return lax.ppermute(array, ("tm", "cells", "feat"), pairs)


def swapped(array, swap):
    cores = lax.axis_size("feat")
    return lax.ppermute(array, "feat", [(core, (core + swap) % cores) for core in range(cores)])


def on_device(principal_coordinates, present_potentials, destination_tiles, living_totals):
    _, feat_count, row_count = principal_coordinates.shape
    _, source_count, list_len = destination_tiles.shape
    block_len = row_count // source_count
    offset = 2.0 / spread - math.log(2 * list_len * block_len)
    times = lax.axis_size("tm")
    row = jax.ShapeDtypeStruct((1, row_count), jnp.float32)
    sums = jax.ShapeDtypeStruct((row_count, lanes), jnp.float32)
    payload_rows = (feat_count + 4) * row_count // lanes
    smem, vmem = pltpu.SMEM, pltpu.VMEM

    scratch = [
        smem(living_totals.shape, jnp.int32),
        vmem(principal_coordinates.shape, bf16),
        vmem(present_potentials.shape, jnp.float32),
        vmem(destination_tiles.shape, jnp.int32),
        pltpu.SemaphoreType.DMA((feat_copies + 3,)),
    ]

    def in_hbm(*arrays):
        return [pltpu.with_memory_space_constraint(array, pltpu.HBM) for array in arrays]

    def packed(weights):
        return call(
            functools.partial(pack_kernel, offset),
            "pack_cells",
            (
                jax.ShapeDtypeStruct((payload_rows, lanes), bf16),
                jax.ShapeDtypeStruct((feat_count * row_count // lanes + list_rows, lanes), bf16),
                jax.ShapeDtypeStruct((8, row_count), jnp.float32),
            ),
            in_hbm(living_totals, principal_coordinates, weights, destination_tiles),
            [pltpu.HBM] * 4,
            scratch,
        )

    count, cores = lax.axis_size("cells"), lax.axis_size("feat")
    xor = count > 1 and count & (count - 1) == 0

    def shifted(distance):
        return lambda place: place ^ distance if xor else (place + distance) % count

    def group_of(distance, swap=0):
        place, core = lax.axis_index("cells"), lax.axis_index("feat")
        source = jnp.bitwise_xor(place, distance) if xor else lax.rem(place + count - distance, count)
        return source * cores + lax.rem(core + cores - swap, cores)

    list_shape = (source_count, list_len, feat_count)
    rows_shape = jax.ShapeDtypeStruct((row_count + list_rows, lanes), bf16)

    def cell_rows(payload):
        return call(functools.partial(rows_kernel, list_shape), "cell_rows", rows_shape, [payload])

    def summed(pack, step):
        payload, near_payload, _ = pack
        forward = None if step is None else step > 0
        moves = (1, -1) if step is None else (step,)
        *distances, far = range(0, count, 2 if xor else 1)
        far_shard = exchange(payload, (moves, shifted(far)))
        shards = {distance: exchange(payload, (moves, shifted(distance))) for distance in distances}

        def added(jobs, cells, ours, total=None, finished=False, built=False):
            result = row if finished else sums
            return call(
                functools.partial(
                    sum_kernel,
                    [there for _, there in jobs],
                    ours,
                    forward,
                    list_shape,
                    built,
                    total is not None,
                    finished,
                ),
                "sum_tiles",
                (rows_shape, result) if built else result,
                [*(shard for shard, _ in jobs), cells] + ([] if total is None else [total]),
                scratch=[
                    smem((len(jobs) * source_count**2 + pairs_at_once,), jnp.int32),
                    vmem((len(jobs) * (feat_count + 16) * row_count // lanes, lanes), bf16),
                    vmem((row_count + block_len, lanes), jnp.float32),
                ],
                exps=len(jobs) * row_count * row_count,
            )

        def job(shard, distance, swap):
            return swapped(shard, swap) if swap else shard, functools.partial(group_of, distance, swap)

        def batch(swap):
            return [job(shard, distance, swap) for distance, shard in shards.items()]

        own = cell_rows(payload)
        if not xor:
            jobs = [one for swap in range(cores) for one in batch(swap)]
            jobs += [job(far_shard, far, swap) for swap in range(cores)]
            return [added(jobs, own, group_of_own, finished=True)]

        near_group = functools.partial(group_of, 1)
        near = exchange(near_payload, ((0,), shifted(1)))
        ready, _ = lax.optimization_barrier((far_shard, own))
        direct = [job(far_shard, far, 0), *batch(0)]
        crossed = [job(ready, far, swap) for swap in range(1, cores)]
        crossed += [one for swap in range(1, cores) for one in batch(swap)]
        near, total = added(direct, near, near_group, built=True)
        total = added(crossed, near, near_group, total, finished=True)
        own, _ = lax.optimization_barrier((own, total))
        return [
            exchange(total, ((0,), shifted(1))),
            added([*direct, *crossed], own, group_of_own, finished=True),
        ]

    group_of_own = functools.partial(group_of, 0)

    if times == 2:
        pack = packed(present_potentials)
        parts = summed(pack, None)
        return tuple(
            call(functools.partial(end_kernel, len(parts)), "end", (row, row), [pack[2], *parts])
        )

    time_here = lax.axis_index("tm")

    def advance(_, state):
        forward, backward = state
        pushed = sum(summed(packed(present_potentials * forward), 1))
        pulled = sum(summed(packed(present_potentials * backward), -1))
        return (
            jnp.where(time_here == 0, 1.0, pushed),
            jnp.where(time_here == times - 1, 1.0, pulled),
        )

    unit = jnp.ones((1, row_count), jnp.float32)
    forward, backward = lax.fori_loop(0, times - 1, advance, (unit, unit))
    return updated(living_totals[time_here].astype(jnp.float32), present_potentials, present_potentials * forward * backward)


def solution(mesh):
    in_specs = (
        P(("runs", "tm"), None, ("cells", "feat")),
        P(("runs", "tm"), ("cells", "feat")),
        P(("runs", "tm"), ("cells", "feat"), None),
        P("runs"),
    )
    out_specs = (P(("runs", "tm"), ("cells", "feat")), P(("runs", "tm"), ("cells", "feat")))
    return jax.shard_map(
        on_device, mesh=mesh, in_specs=in_specs, out_specs=out_specs, check_vma=False
    )
```

```python
import functools
import math

import jax
import jax.numpy as jnp
from jax import lax
from jax.experimental import pallas as pl
from jax.experimental.pallas import tpu as pltpu
from jax.sharding import PartitionSpec as P

spread = 0.5
dead_exponent = -32768.0
vmem_bytes = 32 * 1024 * 1024
lanes = 128
list_rows = 16
pairs_at_once = 6
feat_copies = 4
bf16 = jnp.bfloat16


def pieces(value):
    high = value.astype(bf16).astype(jnp.float32)
    rest = value - high
    mid = rest.astype(bf16).astype(jnp.float32)
    return high, mid, (rest - mid).astype(bf16).astype(jnp.float32)


def stacked_rows(rows, height, width):
    row_ids = lax.broadcasted_iota(jnp.int32, (height, width), 0)
    block = jnp.zeros((height, width), jnp.float32)
    for place, row in enumerate(rows):
        block = jnp.where(row_ids == place, row, block)
    return block


def lane_blocks(row):
    return jnp.concatenate(
        [row[:, start : start + lanes] for start in range(0, row.shape[1], lanes)], axis=0
    )


def here():
    return lax.axis_index("cells") * lax.axis_size("feat") + lax.axis_index("feat")


def listed_row(lists):
    source_count, list_len = lists.shape
    rows = [lists[place : place + 1] for place in range(source_count)]
    fill = jnp.full((1, lanes - source_count * list_len), -1.0, jnp.float32)
    return jnp.concatenate(rows + [fill], axis=1)


def fetch(sources, targets, sems):
    copies = [
        pltpu.make_async_copy(source, target, sems.at[place])
        for place, (source, target) in enumerate(zip(sources, targets))
    ]
    for copy in copies:
        copy.start()
    for copy in copies:
        copy.wait()


def pack_kernel(
    offset, totals_hbm, feats_hbm, weights_hbm, lists_hbm, payload_ref, near_ref, facts_ref, *scratch
):
    totals_ref, feats_ref, weights_ref, lists_ref, sems = scratch
    _, feat_count, row_count = feats_ref.shape
    share = feat_count // feat_copies
    parts = [pl.ds(start, share) for start in range(0, feat_count, share)]
    fetch(
        [*(feats_hbm.at[:, part, :] for part in parts), weights_hbm, lists_hbm, totals_hbm],
        [*(feats_ref.at[:, part, :] for part in parts), weights_ref, lists_ref, totals_ref],
        sems,
    )
    _, source_count, _ = lists_ref.shape
    slabs = row_count // lanes
    feats = feats_ref[0]
    wide = feats.astype(jnp.float32)
    squares = lane_blocks(jnp.sum(wide * wide, axis=0, keepdims=True)) / (spread * feat_count)
    shape = (slabs, lanes)
    positions = here() * row_count + lanes * lax.broadcasted_iota(jnp.int32, shape, 0)
    positions = positions + lax.broadcasted_iota(jnp.int32, shape, 1)
    weights = lane_blocks(weights_ref[...])
    alive = totals_ref[lax.axis_index("tm")]
    used = (positions < alive) & (weights > 1e-37)
    share = offset - squares + jnp.log(jnp.where(used, weights, 1.0))
    share = jnp.where(used, share, dead_exponent)
    listed = jnp.broadcast_to(listed_row(lists_ref[0].astype(jnp.float32)), shape)
    tail = jnp.concatenate([*pieces(share), listed], axis=0).astype(bf16)
    columns = [feats[:, slab * lanes : (slab + 1) * lanes] for slab in range(slabs)]
    payload_ref[...] = jnp.concatenate([*columns, tail], axis=0)
    near_tail = jnp.broadcast_to(listed[:1], (list_rows, lanes)).astype(bf16)
    near_ref[...] = jnp.concatenate([*columns, near_tail], axis=0)
    facts_ref[...] = stacked_rows([weights_ref[...], alive.astype(jnp.float32)], 8, row_count)


def rows_kernel(list_shape, payload_ref, rows_ref):
    source_count, _, feat_count = list_shape
    row_count = rows_ref.shape[0] - list_rows
    slabs = row_count // lanes
    feats = [payload_ref[slab * feat_count : (slab + 1) * feat_count, :] for slab in range(slabs)]
    wide = jnp.concatenate(feats, axis=1).astype(jnp.float32)
    squares = jnp.sum(wide * wide, axis=0, keepdims=True) / (spread * feat_count)
    block = lax.broadcasted_iota(jnp.int32, (1, row_count), 1) // (row_count // source_count)
    member = [jnp.where(block == place, 1.0, 0.0) for place in range(source_count)]
    tail = stacked_rows(
        [1.0, 1.0, 1.0, *pieces(-squares), 0.0, 0.0, *member], lanes - feat_count, row_count
    )
    columns = jnp.concatenate([wide * (2.0 / (spread * feat_count)), tail], axis=0)
    rows_ref[:row_count, :] = columns.T.astype(bf16)
    height = payload_ref.shape[0]
    listed = payload_ref[height - list_rows :, :].astype(jnp.float32)[list_rows - 1 :]
    rows_ref[row_count:, :] = jnp.broadcast_to(listed, (list_rows, lanes)).astype(bf16)


def updated(alive, potentials, prior):
    _, row_count = potentials.shape
    positions = here() * row_count + lax.broadcasted_iota(jnp.int32, (1, row_count), 1)
    live = positions.astype(jnp.float32) < alive
    prior = jnp.where(live, prior, 0.0)
    cell_total = row_count * lax.axis_size("cells") * lax.axis_size("feat")
    wanted = cell_total / alive
    scales = potentials * jnp.sqrt(wanted / jnp.where(live, prior, 1.0))
    return jnp.where(live, scales, 0.0), prior


def listed_pairs(tails, own_lists, ours, groups, forward, list_shape):
    source_count, list_len, _ = list_shape
    by_sender = lax.axis_index("tm") > 0 if forward is None else jnp.bool_(forward)
    lister = lax.broadcasted_iota(jnp.int32, (1, lanes), 1) // list_len
    found = jnp.zeros((1, lanes), jnp.int32)
    for shard, (sent, there) in enumerate(zip(tails, groups)):
        values = jnp.where(by_sender, sent, own_lists)
        first = jnp.where(by_sender, ours, there) * source_count
        for place in range(source_count):
            bit = jnp.where(by_sender, place * source_count + lister, lister * source_count + place)
            bit = bit + shard * source_count**2
            hit = values == (first + place).astype(jnp.float32)
            found = found + jnp.where(hit, jnp.left_shift(1, bit), 0)
    return jnp.sum(found)


def sum_pairs(shards, groups, rows_ref, ours, forward, list_shape, list_ref, tiles_ref, total_ref):
    source_count, _, feat_count = list_shape
    row_count = rows_ref.shape[0] - list_rows
    block_len = row_count // source_count
    slabs = row_count // lanes
    depth = feat_count + 16
    own_lists = rows_ref[row_count:, :].astype(jnp.float32)[:1]
    tails = []
    for place, shard_ref in enumerate(shards):
        tail = shard_ref[slabs * feat_count :, :].astype(jnp.float32)
        tails.append(tail[3 * slabs : 3 * slabs + 1])
        for slab in range(slabs):
            share = [tail[piece * slabs + slab : piece * slabs + slab + 1] for piece in range(3)]
            rows = stacked_rows([*share, 1.0, 1.0, 1.0], 16, lanes).astype(bf16)
            feats = shard_ref[slab * feat_count : (slab + 1) * feat_count, :]
            start = (place * slabs + slab) * depth
            tiles_ref[start : start + depth, :] = jnp.concatenate([feats, rows], axis=0)
    square = source_count**2
    at_once = 32 // square
    count = jnp.int32(0)
    for first in range(0, len(shards), at_once):
        last = min(first + at_once, len(shards))
        bits = listed_pairs(tails[first:last], own_lists, ours, groups[first:last], forward, list_shape)
        for place in range((last - first) * square):
            list_ref[count] = jnp.int32(first * square + place)
            count = count + jnp.bitwise_and(jnp.right_shift(bits, place), 1)
    pair_total = len(shards) * square
    for place in range(pairs_at_once - 1):
        list_ref[count + place] = jnp.int32(pair_total)

    def step(taken, size):
        sums = []
        for place in range(size):
            listed = list_ref[taken + place]
            pair = jnp.minimum(listed, pair_total - 1)
            block, other = lax.rem(pair // source_count, source_count), lax.rem(pair, source_count)
            row = pl.multiple_of(block * block_len, block_len)
            tile = (pair // square * source_count + other) * (slabs // source_count) * depth
            columns = [
                tiles_ref[pl.ds(pl.multiple_of(tile + slab * depth, 16), depth), :]
                for slab in range(slabs // source_count)
            ]
            exponents = jnp.dot(
                rows_ref[pl.ds(row, block_len), :depth],
                jnp.concatenate(columns, axis=1),
                preferred_element_type=jnp.float32,
            )
            terms = jnp.exp(exponents)
            added = terms[:, :lanes]
            for start in range(lanes, block_len, lanes):
                added = added + terms[:, start : start + lanes]
            sums.append((jnp.where(listed < pair_total, row, row_count), added))
        for row, added in sums:
            total_ref[pl.ds(pl.multiple_of(row, block_len), block_len), :] += added

    def whole_step(index, carry):
        step(index * pairs_at_once, pairs_at_once)
        return carry

    half = pairs_at_once // 2
    whole_steps = (count + pairs_at_once - 1 - half) // pairs_at_once
    lax.fori_loop(0, whole_steps, whole_step, 0)

    @pl.when(count > whole_steps * pairs_at_once)
    def _():
        step(whole_steps * pairs_at_once, half)


def sum_kernel(groups, ours, forward, list_shape, built, started, finished, *refs):
    *refs, list_ref, tiles_ref, total_ref = refs
    shards, (cells_ref, *refs) = refs[: len(groups)], refs[len(groups) :]
    rows_ref = cells_ref
    if built:
        rows_ref, *refs = refs
        rows_kernel(list_shape, cells_ref, rows_ref)
    row_count = rows_ref.shape[0] - list_rows
    if started:
        total_ref[:row_count, :], refs = refs[0][...], refs[1:]
    else:
        total_ref[:row_count, :] = jnp.zeros((row_count, lanes), jnp.float32)
    theres = [there() for there in groups]
    sum_pairs(shards, theres, rows_ref, ours(), forward, list_shape, list_ref, tiles_ref, total_ref)
    total = total_ref[:row_count, :]
    refs[0][...] = jnp.sum(total.T, axis=0, keepdims=True) if finished else total


def end_kernel(parts, facts_ref, *refs):
    message = refs[0][...]
    for part_ref in refs[1:parts]:
        message = message + part_ref[...]
    scales_ref, prior_ref = refs[parts:]
    potentials = facts_ref[0:1]
    scales_ref[...], prior_ref[...] = updated(facts_ref[1:2], potentials, potentials * message)


def call(kernel, name, out_shapes, operands, spaces=None, scratch=(), exps=0):
    spaces = spaces or [pltpu.VMEM] * len(operands)
    return pl.pallas_call(
        kernel,
        name=name,
        out_shape=out_shapes,
        in_specs=[pl.BlockSpec(memory_space=space) for space in spaces],
        out_specs=jax.tree.map(lambda _: pl.BlockSpec(memory_space=pltpu.VMEM), out_shapes),
        scratch_shapes=scratch,
        compiler_params=pltpu.CompilerParams(vmem_limit_bytes=vmem_bytes),
        cost_estimate=pl.CostEstimate(flops=160 * exps, bytes_accessed=2**17, transcendentals=exps),
    )(*operands)


def exchange(array, route):
    (moves, shift) = route
    times, count, cores = lax.axis_size("tm"), lax.axis_size("cells"), lax.axis_size("feat")
    pairs = [
        ((time * count + place) * cores + core, ((time + move) * count + shift(place)) * cores + core)
        for time in range(times)
        for move in moves
        if 0 <= time + move < times
        for place in range(count)
        for core in range(cores)
    ]
    return lax.ppermute(array, ("tm", "cells", "feat"), pairs)


def swapped(array, swap):
    cores = lax.axis_size("feat")
    return lax.ppermute(array, "feat", [(core, (core + swap) % cores) for core in range(cores)])


def on_device(principal_coordinates, present_potentials, destination_tiles, living_totals):
    _, feat_count, row_count = principal_coordinates.shape
    _, source_count, list_len = destination_tiles.shape
    block_len = row_count // source_count
    offset = 2.0 / spread - math.log(2 * list_len * block_len)
    times = lax.axis_size("tm")
    row = jax.ShapeDtypeStruct((1, row_count), jnp.float32)
    sums = jax.ShapeDtypeStruct((row_count, lanes), jnp.float32)
    payload_rows = (feat_count + 4) * row_count // lanes
    smem, vmem = pltpu.SMEM, pltpu.VMEM

    scratch = [
        smem(living_totals.shape, jnp.int32),
        vmem(principal_coordinates.shape, bf16),
        vmem(present_potentials.shape, jnp.float32),
        vmem(destination_tiles.shape, jnp.int32),
        pltpu.SemaphoreType.DMA((feat_copies + 3,)),
    ]

    def in_hbm(*arrays):
        return [pltpu.with_memory_space_constraint(array, pltpu.HBM) for array in arrays]

    def packed(weights):
        return call(
            functools.partial(pack_kernel, offset),
            "pack_cells",
            (
                jax.ShapeDtypeStruct((payload_rows, lanes), bf16),
                jax.ShapeDtypeStruct((feat_count * row_count // lanes + list_rows, lanes), bf16),
                jax.ShapeDtypeStruct((8, row_count), jnp.float32),
            ),
            in_hbm(living_totals, principal_coordinates, weights, destination_tiles),
            [pltpu.HBM] * 4,
            scratch,
        )

    count, cores = lax.axis_size("cells"), lax.axis_size("feat")
    xor = count > 1 and count & (count - 1) == 0

    def shifted(distance):
        return lambda place: place ^ distance if xor else (place + distance) % count

    def group_of(distance, swap=0):
        place, core = lax.axis_index("cells"), lax.axis_index("feat")
        source = jnp.bitwise_xor(place, distance) if xor else lax.rem(place + count - distance, count)
        return source * cores + lax.rem(core + cores - swap, cores)

    list_shape = (source_count, list_len, feat_count)
    rows_shape = jax.ShapeDtypeStruct((row_count + list_rows, lanes), bf16)

    def cell_rows(payload):
        return call(functools.partial(rows_kernel, list_shape), "cell_rows", rows_shape, [payload])

    def summed(pack, step):
        payload, near_payload, _ = pack
        forward = None if step is None else step > 0
        moves = (1, -1) if step is None else (step,)
        *distances, far = range(0, count, 2 if xor else 1)
        far_shard = exchange(payload, (moves, shifted(far)))
        shards = {distance: exchange(payload, (moves, shifted(distance))) for distance in distances}

        def added(jobs, cells, ours, total=None, finished=False, built=False):
            result = row if finished else sums
            return call(
                functools.partial(
                    sum_kernel,
                    [there for _, there in jobs],
                    ours,
                    forward,
                    list_shape,
                    built,
                    total is not None,
                    finished,
                ),
                "sum_tiles",
                (rows_shape, result) if built else result,
                [*(shard for shard, _ in jobs), cells] + ([] if total is None else [total]),
                scratch=[
                    smem((len(jobs) * source_count**2 + pairs_at_once,), jnp.int32),
                    vmem((len(jobs) * (feat_count + 16) * row_count // lanes, lanes), bf16),
                    vmem((row_count + block_len, lanes), jnp.float32),
                ],
                exps=len(jobs) * row_count * row_count,
            )

        def job(shard, distance, swap):
            return swapped(shard, swap) if swap else shard, functools.partial(group_of, distance, swap)

        def batch(swap):
            return [job(shard, distance, swap) for distance, shard in shards.items()]

        own = cell_rows(payload)
        if not xor:
            jobs = [one for swap in range(cores) for one in batch(swap)]
            jobs += [job(far_shard, far, swap) for swap in range(cores)]
            return [added(jobs, own, group_of_own, finished=True)]

        near_group = functools.partial(group_of, 1)
        near = exchange(near_payload, ((0,), shifted(1)))
        ready, _ = lax.optimization_barrier((far_shard, own))
        direct = [job(far_shard, far, 0), *batch(0)]
        crossed = [job(ready, far, swap) for swap in range(1, cores)]
        crossed += [one for swap in range(1, cores) for one in batch(swap)]
        near, total = added(direct, near, near_group, built=True)
        total = added(crossed, near, near_group, total, finished=True)
        own, _ = lax.optimization_barrier((own, total))
        return [
            exchange(total, ((0,), shifted(1))),
            added([*direct, *crossed], own, group_of_own, finished=True),
        ]

    group_of_own = functools.partial(group_of, 0)

    if times == 2:
        pack = packed(present_potentials)
        parts = summed(pack, None)
        return tuple(
            call(functools.partial(end_kernel, len(parts)), "end", (row, row), [pack[2], *parts])
        )

    time_here = lax.axis_index("tm")

    def advance(_, state):
        forward, backward = state
        pushed = sum(summed(packed(present_potentials * forward), 1))
        pulled = sum(summed(packed(present_potentials * backward), -1))
        return (
            jnp.where(time_here == 0, 1.0, pushed),
            jnp.where(time_here == times - 1, 1.0, pulled),
        )

    unit = jnp.ones((1, row_count), jnp.float32)
    forward, backward = lax.fori_loop(0, times - 1, advance, (unit, unit))
    return updated(living_totals[time_here].astype(jnp.float32), present_potentials, present_potentials * forward * backward)


def solution(mesh):
    in_specs = (
        P(("runs", "tm"), None, ("cells", "feat")),
        P(("runs", "tm"), ("cells", "feat")),
        P(("runs", "tm"), ("cells", "feat"), None),
        P("runs"),
    )
    out_specs = (P(("runs", "tm"), ("cells", "feat")), P(("runs", "tm"), ("cells", "feat")))
    return jax.shard_map(
        on_device, mesh=mesh, in_specs=in_specs, out_specs=out_specs, check_vma=False
    )
```
